128 devices in a mesh: comp: 2 (over z_lo), tile: 64 (over x, y, z_hi, core).
Axes of the slice: x: 4, y: 4, z: 4 (z_hi: 2, z_lo: 2; z = z_hi * 2 + z_lo), core: 2. Of those that a mesh axis runs over, the one named last changes fastest.
Arguments:
- state: float32 [2, 2, 64, 4096, 256], P('comp', None, None, 'tile'), may hold values from -6 to 6
- horiz_rate: float32 [2, 2, 64], P('comp'), may hold values from 0.02 to 0.2
- vert_rate: float32 [2, 2], P('comp'), may hold values from 0.02 to 0.15
- sea_mask: int32 [4096, 256], P('tile'), may hold values 0 or 1
- exchange_coef: float32 [4096, 256], P('tile'), may hold values from 0.1 to 0.5
- partner: int32 [64], replicated, may hold values from 0 to 63, each once
Outputs:
- new_state: float32 [2, 2, 64, 4096, 256], P('comp', None, None, 'tile')
The draws below stay inside these ranges and needn't reach their ends.
Inputs may be any that keep to these rules, and one draw needn't show every extreme that they name: `partner`: each tile number appears once.
All inputs are finite; a program needn't handle non-finite values. No bound on the sum of `sea_mask` on one device may be relied on, other than what follows from the above.
Results may differ from the reference program's by a relative error of at most 0.00002.
Values sent between devices are 32-bit elements; how exact they have to be, the bound alone decides.
No kernel may reach another device: no remote copies, remote signals or barrier semaphores. Data moves between devices by JAX's collectives and lax.ppermute only.
A program may use at most 128 MiB of HBM per device.

```python
import math
import jax
import jax.numpy as jnp

NY = 256
LEV = 64
FIELDS = 2
STEPS = 2
TILES = 64
NX = 4096


def touch_ends(entries, key, low, high):
    extent = entries.shape
    place = [jax.random.randint(jax.random.fold_in(key, axis), (), 0, extent[axis]) for axis in range(len(extent))]
    entries = entries.at[tuple(place)].set(low)
    longest = extent.index(max(extent))
    place[longest] = (place[longest] + 1) % extent[longest]
    return entries.at[tuple(place)].set(high)


def levels(stream_key, extent, pieces, least, high):
    level, own = 1.0, jax.random.fold_in(stream_key, 6)
    for axis_at, parts in pieces:
        heights = jnp.exp(jax.random.uniform(jax.random.fold_in(own, axis_at), (parts,), jnp.float32, least / len(pieces), high / len(pieces)))
        level = level * jnp.repeat(heights, extent[axis_at] // parts).reshape([-1 if axis == axis_at else 1 for axis in range(len(extent))])
    return level


def centred(own_key, shape, scale, limit, shards=(), dtype=jnp.bfloat16):
    values = scale * jax.random.normal(own_key, shape, jnp.float32)
    if shards:
        values = values * levels(own_key, shape, shards, -0.22, 0.18)
    return jnp.clip(values, -limit, limit).astype(dtype)


def setup_inputs(seed: int = 0) -> dict:
    arg_keys = jax.random.split(jax.random.key(seed), 7)
    state = centred(arg_keys[0], (2, FIELDS, LEV, NX, NY), 1.0, 6.0, ((0, 2), (3, 64)), jnp.float32)
    horiz_rate = jnp.clip(jnp.exp(math.log(0.2) - 2.3025851 * jax.random.uniform(arg_keys[1], (2, FIELDS, LEV), jnp.float32) ** levels(arg_keys[1], (2, FIELDS, LEV), ((0, 2),), -0.2, 0.2)), 0.02, 0.2)
    vert_rate = jnp.clip(jnp.exp(math.log(0.15) - 2.014903 * jax.random.uniform(arg_keys[2], (2, FIELDS), jnp.float32) ** levels(arg_keys[2], (2, FIELDS), ((0, 2),), -0.2, 0.2)), 0.02, 0.15)
    sea_mask = touch_ends((jax.random.randint(arg_keys[3], (NX, NY), 0, 4) < 3).astype(jnp.int32), jax.random.fold_in(arg_keys[3], 1), 0, 1)
    exchange_coef = jnp.clip(jnp.exp(math.log(0.5) - 1.609438 * jax.random.uniform(arg_keys[4], (NX, NY), jnp.float32) ** levels(arg_keys[4], (NX, NY), ((0, 64),), -0.2, 0.2)), 0.1, 0.5)
    partner = jax.random.permutation(arg_keys[5], TILES).astype(jnp.int32)
    return dict(state=state, horiz_rate=horiz_rate, vert_rate=vert_rate, sea_mask=sea_mask, exchange_coef=exchange_coef, partner=partner)


def mix_once(fields, horiz, vert, scale):
    lap = jnp.roll(fields, -1, -2) + jnp.roll(fields, 1, -2) + jnp.roll(fields, 1, -1) + jnp.roll(fields, -1, -1) - 4.0 * fields
    above = jnp.concatenate([fields[:, 1:], fields[:, -1:]], 1)
    below = jnp.concatenate([fields[:, :1], fields[:, :-1]], 1)
    vlap = above + below - 2.0 * fields
    fields = fields + horiz[:, :, None, None] * lap + vert[:, None, None, None] * vlap
    return fields * scale


def reference(state, horiz_rate, vert_rate, sea_mask, exchange_coef, partner):
    tiles = partner.shape[0]
    rows = state.shape[3] // tiles
    width = state.shape[4]
    inverse = jnp.argsort(partner).astype(jnp.int32)
    atm_surf = state[0, 0, 0].reshape(tiles, rows, width)
    ocn_surf = state[1, 0, 0].reshape(tiles, rows, width)
    sea = sea_mask.astype(jnp.float32).reshape(tiles, rows, width)
    coef = exchange_coef.reshape(tiles, rows, width)
    flux = coef * (atm_surf - ocn_surf[partner]) * sea[partner]
    ocn_flux = flux[inverse]
    atm_new = (atm_surf - flux).reshape(-1, width)
    ocn_new = (ocn_surf + ocn_flux).reshape(-1, width)
    atm = state[0].at[0, 0].set(atm_new)
    ocn = state[1].at[0, 0].set(ocn_new)
    seaf = sea_mask.astype(jnp.float32)
    for step in range(STEPS):
        atm = mix_once(atm, horiz_rate[0], vert_rate[0], jnp.float32(1.0))
        ocn = mix_once(ocn, horiz_rate[1], vert_rate[1], seaf)
    return jnp.stack([atm, ocn])
```

```python
import functools

import jax
import jax.numpy as jnp
from jax import lax
from jax.experimental import pallas as pl
from jax.experimental.pallas import tpu as pltpu
from jax.sharding import PartitionSpec as P

BOTH = ("comp", "tile")
CHUNK = 8
MIB = 1 << 20


def row_ids(rows, width):
    return lax.broadcasted_iota(jnp.int32, (rows, width), 0)


def beside(x):
    width = x.shape[-1]
    return pltpu.roll(x, 1, 1) + pltpu.roll(x, width - 1, 1)


def around(groups, before, after, top, bottom):
    down = [pltpu.roll(x, 1, 0) for x in groups]
    up = [pltpu.roll(x, 7, 0) for x in groups]
    down_edge = [jnp.broadcast_to(before, groups[0].shape)] + down[:-1]
    up_edge = up[1:] + [jnp.broadcast_to(after, groups[0].shape)]
    return [
        (jnp.where(top, de, d) + jnp.where(bottom, ue, u)) + beside(x)
        for x, d, de, u, ue in zip(groups, down, down_edge, up, up_edge)
    ]


def mix_kernel(hz, vt, state, mine_first, mine_last, before, after, mask, hcol, dep, out, base, raw, s1, res, edge, in_sem, out_sem):
    del dep
    fields, levels, rows, width = state.shape
    per = levels // CHUNK
    total = fields * per

    def load(q):
        f, c = q // per, q % per
        where = (f, pl.ds(c * CHUNK, CHUNK))
        return pltpu.make_async_copy(state.at[where], raw.at[where], in_sem.at[q])

    def store(q):
        f, c = q // per, q % per
        where = (f, pl.ds(c * CHUNK, CHUNK))
        return pltpu.make_async_copy(res.at[where], out.at[where], out_sem.at[q])

    @pl.loop(0, total)
    def _(q):
        load(q).start()

    planes = fields * levels
    level = row_ids(levels, width)
    for side, (x2, x1, x0, m) in enumerate(
        (
            (before.at[0], before.at[1], mine_first.at[0], before[1, planes : planes + 1, :]),
            (after.at[1], after.at[0], mine_last.at[1], after[0, planes : planes + 1, :]),
        )
    ):
        for f in range(fields):
            at = pl.ds(f * levels, levels)
            x = x1[at, :]
            lap = x2[at, :] + x0[at, :] + beside(x)
            below = jnp.where(level == 0, x, pltpu.roll(x, 1, 0))
            above = jnp.where(level == levels - 1, x, pltpu.roll(x, levels - 1, 0))
            h = hcol[at, :]
            v = vt[f]
            new = x * (1.0 - 4.0 * h - 2.0 * v) + h * lap + v * (above + below)
            edge[side, at, :] = new * m

    row = row_ids(8, width)
    top, bottom = row == 0, row == 7
    ngroups = rows // 8

    def split(ref, f, l):
        return [ref[f, l, pl.ds(8 * g, 8), :] for g in range(ngroups)]

    def substep(src, dst, f, l, ahead, behind):
        h, v = hz[f, l], vt[f]
        c0 = 1.0 - 4.0 * h - 2.0 * v
        lo, hi = jnp.maximum(l - 1, 0), jnp.minimum(l + 1, levels - 1)
        x = split(src, f, l)
        p = f * levels + l
        lap = around(x, ahead[pl.ds(p, 1), :], behind[pl.ds(p, 1), :], top, bottom)
        for g in range(ngroups):
            at = pl.ds(8 * g, 8)
            vert = src[f, lo, at, :] + src[f, hi, at, :]
            dst[f, l, at, :] = (x[g] * c0 + h * lap[g] + v * vert) * mask[at, :]

    def first(f, l):
        substep(raw, s1, f, l, before.at[1], after.at[0])

    def second(f, l):
        substep(s1, res, f, l, edge.at[0], edge.at[1])

    @pl.loop(0, total)
    def _(q):
        f, c = q // per, q % per

        @pl.when(c == 0)
        def _():
            load(q).wait()
            first(f, 0)

        @pl.when(c < per - 1)
        def _():
            load(q + 1).wait()

        @pl.loop(0, CHUNK, unroll=2)
        def _(i):
            l = c * CHUNK + i
            first(f, jnp.minimum(l + 1, levels - 1))
            second(f, l)

        store(q).start()

        @pl.when(q == 0)
        def _():
            base[...] = res[0, 0:3]

    @pl.loop(0, total)
    def _(q):
        store(q).wait()


def mix(fields, hz, vt, first, last, before, after, mask, dep):
    nf, levels, rows, width = fields.shape
    planes = nf * levels
    vmem = pl.BlockSpec(memory_space=pltpu.VMEM)
    smem = pl.BlockSpec(memory_space=pltpu.SMEM)
    anyw = pl.BlockSpec(memory_space=pl.ANY)
    total = nf * levels // CHUNK
    return pl.pallas_call(
        mix_kernel,
        out_shape=(
            jax.ShapeDtypeStruct(fields.shape, jnp.float32),
            jax.ShapeDtypeStruct((3, rows, width), jnp.float32),
        ),
        in_specs=[smem, smem, anyw, vmem, vmem, vmem, vmem, vmem, vmem, anyw],
        out_specs=(anyw, vmem),
        scratch_shapes=[
            pltpu.VMEM(fields.shape, jnp.float32),
            pltpu.VMEM(fields.shape, jnp.float32),
            pltpu.VMEM(fields.shape, jnp.float32),
            pltpu.VMEM((2, planes, width), jnp.float32),
            pltpu.SemaphoreType.DMA((total,)),
            pltpu.SemaphoreType.DMA((total,)),
        ],
        compiler_params=pltpu.CompilerParams(vmem_limit_bytes=40 * MIB),
        cost_estimate=pl.CostEstimate(flops=26 * fields.size, bytes_accessed=8 * fields.size, transcendentals=0),
        name="mix",
    )(hz, vt, fields, first, last, before, after, mask, hz.reshape(planes, 1), dep)


def flux_kernel(partner, place, got, back, theirs, turned):
    tiles = got.shape[0] // 2
    half = got.shape[1] // 2
    for t in range(tiles):
        theirs[t : t + 1, :] = got[pl.ds(tiles + partner[t], 1), :]
    flux = got[0:tiles, half:] * (got[0:tiles, 0:half] - theirs[:, 0:half]) * theirs[:, half:]
    back[0:tiles, 0:half] = flux
    for t in range(tiles):
        turned[pl.ds(partner[t], 1), :] = back[t : t + 1, 0:half]
    other = turned[...]
    back[tiles:, 0:half] = other
    near_start = place[0] < 2

    @pl.when(near_start)
    def _():
        back[0:tiles, half:] = pltpu.roll(flux, tiles - 1, 0)
        back[tiles:, half:] = pltpu.roll(other, tiles - 1, 0)

    @pl.when(jnp.logical_not(near_start))
    def _():
        back[0:tiles, half:] = pltpu.roll(flux, 1, 0)
        back[tiles:, half:] = pltpu.roll(other, 1, 0)


def flux_pieces(partner, place, got):
    vmem = pl.BlockSpec(memory_space=pltpu.VMEM)
    smem = pl.BlockSpec(memory_space=pltpu.SMEM)
    tiles, half = got.shape[0] // 2, got.shape[1] // 2
    return pl.pallas_call(
        flux_kernel,
        out_shape=jax.ShapeDtypeStruct(got.shape, jnp.float32),
        in_specs=[smem, smem, vmem],
        out_specs=vmem,
        scratch_shapes=[pltpu.VMEM((tiles, 2 * half), jnp.float32), pltpu.VMEM((tiles, half), jnp.float32)],
        cost_estimate=pl.CostEstimate(flops=4 * got.size, bytes_accessed=8 * got.size, transcendentals=0),
        name="flux",
    )(partner, place, got)


def add_kernel(hz, vt, sign, base, back, mask, medge, whole, out, ext, three, sem):
    del whole
    rows, width = mask.shape
    half = width // 2
    v, s = vt[0], sign[0]
    zero_pad = jnp.zeros((8, width), jnp.float32)
    ext[0:8, :] = zero_pad
    ext[8 + rows : 16 + rows, :] = zero_pad
    for k in range(2):
        lanes = pl.ds(k * half, half)
        ext[8 : 8 + rows, lanes] = back[pl.ds(k * rows, rows), 0:half] * s
        ext[6:8, lanes] = back[pl.ds(k * rows + rows - 2, 2), half:] * s
        ext[8 + rows : 10 + rows, lanes] = back[pl.ds(k * rows, 2), half:] * s

    total = rows + 16
    m = jnp.concatenate(
        [jnp.broadcast_to(medge[0:1, :], (8, width)), mask[...], jnp.broadcast_to(medge[1:2, :], (8, width))], 0
    )

    def lateral(x):
        return pltpu.roll(x, 1, 0) + pltpu.roll(x, total - 1, 0) + beside(x)

    d = ext[...]
    h0, h1 = hz[0, 0], hz[0, 1]
    one0 = m * ((1.0 - 4.0 * h0 - v) * d + h0 * lateral(d))
    one1 = m * (v * d)
    two0 = (1.0 - 4.0 * h0 - v) * one0 + h0 * lateral(one0) + v * one1
    two1 = (1.0 - 4.0 * h1 - 2.0 * v) * one1 + h1 * lateral(one1) + v * one0
    two2 = v * one1
    for level, two in enumerate((two0, two1, two2)):
        three[level] = base[level] + (m * two)[8 : 8 + rows]
    copy = pltpu.make_async_copy(three, out.at[0, pl.ds(0, 3)], sem)
    copy.start()
    copy.wait()


def add_flux(hz, vt, sign, base, back, mask, medge, whole):
    vmem = pl.BlockSpec(memory_space=pltpu.VMEM)
    smem = pl.BlockSpec(memory_space=pltpu.SMEM)
    anyw = pl.BlockSpec(memory_space=pl.ANY)
    rows, width = mask.shape
    return pl.pallas_call(
        add_kernel,
        out_shape=jax.ShapeDtypeStruct(whole.shape, jnp.float32),
        in_specs=[smem, smem, smem, vmem, vmem, vmem, vmem, anyw],
        out_specs=anyw,
        scratch_shapes=[pltpu.VMEM((rows + 16, width), jnp.float32), pltpu.VMEM(base.shape, jnp.float32), pltpu.SemaphoreType.DMA],
        input_output_aliases={7: 0},
        cost_estimate=pl.CostEstimate(flops=30 * mask.size, bytes_accessed=32 * mask.size, transcendentals=0),
        name="add",
    )(hz, vt, sign, base, back, mask, medge, whole)


def halves(plane):
    half = plane.shape[1] // 2
    return jnp.concatenate([plane[:, :half], plane[:, half:]], 0)


def edge_rows(fields, scale, start):
    nf, levels, _, width = fields.shape
    rows = lax.slice_in_dim(fields, start, start + 2, axis=2).transpose(2, 0, 1, 3).reshape(2, nf * levels, width)
    return jnp.concatenate([rows, scale[start : start + 2][:, None]], 1)


def per_device(state, horiz_rate, vert_rate, sea_mask, exchange_coef, partner):
    is_atmos = lax.axis_index("comp") == 0
    ntile = lax.axis_size("tile")
    fields, hz, vt = state[0], horiz_rate[0], vert_rate[0]
    rows = fields.shape[2]
    wet = sea_mask.astype(jnp.float32)
    scale = jnp.where(is_atmos, jnp.ones_like(wet), wet)

    outgoing = jnp.concatenate([halves(fields[0, 0]), halves(jnp.where(is_atmos, exchange_coef, wet))], 1)
    got = lax.all_to_all(outgoing, BOTH, 0, 0, tiled=True)
    place = lax.axis_index("tile").astype(jnp.int32).reshape(1)
    pieces = flux_pieces(partner, place, got)
    back = lax.all_to_all(pieces, BOTH, 0, 0, tiled=True)

    up = [(i, (i + 1) % ntile) for i in range(ntile)]
    down = [(j, i) for i, j in up]
    first, last = edge_rows(fields, scale, 0), edge_rows(fields, scale, rows - 2)
    before, after = lax.ppermute(last, "tile", up), lax.ppermute(first, "tile", down)

    whole, base = mix(fields, hz, vt, first, last, before, after, scale, pieces)
    medge = jnp.concatenate([before[1, -1:], after[0, -1:]], 0)
    sign = jnp.where(is_atmos, -1.0, 1.0).astype(jnp.float32).reshape(1)
    return add_flux(hz, vt, sign, base, back, scale, medge, whole)[None]


def solution(mesh):
    placed = (
        P("comp", None, None, "tile", None),
        P("comp", None, None),
        P("comp", None),
        P("tile", None),
        P("tile", None),
        P(),
    )
    return jax.shard_map(
        per_device,
        mesh=mesh,
        in_specs=placed,
        out_specs=P("comp", None, None, "tile", None),
        check_vma=False,
    )
```

```python
import functools

import jax
import jax.numpy as jnp
from jax import lax
from jax.experimental import pallas as pl
from jax.experimental.pallas import tpu as pltpu
from jax.sharding import PartitionSpec as P

BOTH = ("comp", "tile")
CHUNK = 8
UNROLL = 8
MIB = 1 << 20


def row_ids(rows, width):
    return lax.broadcasted_iota(jnp.int32, (rows, width), 0)


def beside(x):
    half = x.shape[-1] // 2
    a, b = x[:, :half], x[:, half:]
    lane = lax.broadcasted_iota(jnp.int32, a.shape, 1)
    first, last = lane == 0, lane == half - 1
    ra, rb = pltpu.roll(a, 1, 1), pltpu.roll(b, 1, 1)
    la, lb = pltpu.roll(a, half - 1, 1), pltpu.roll(b, half - 1, 1)
    left = jnp.where(first, rb, ra) + jnp.where(last, lb, la)
    right = jnp.where(first, ra, rb) + jnp.where(last, la, lb)
    return jnp.concatenate([left, right], 1)


def mix_kernel(
    place, hz_any, vt_any, state, sent_near, sent_far, got_near, got_far, mask, out, base, aux,
    mine, halo, strip_sem, hz, vt, hcol, raw, s1, res, edge, split, wet, rate_sem, in_sem, out_sem,
):
    fields, levels, rows, width = state.shape
    per = levels // CHUNK
    total = fields * per
    half = width // 2
    sides = [pl.ds(k * half, half) for k in range(2)]

    def load(q):
        f, c = q // per, q % per
        where = (f, pl.ds(c * CHUNK, CHUNK))
        return [
            pltpu.make_async_copy(state.at[(*where, slice(None), lanes)], raw.at[(k, *where)], in_sem.at[q, k])
            for k, lanes in enumerate(sides)
        ]

    def store(q):
        f, c = q // per, q % per
        where = (f, pl.ds(c * CHUNK, CHUNK))
        return [
            pltpu.make_async_copy(res.at[(k, *where)], out.at[(*where, slice(None), lanes)], out_sem.at[q, k])
            for k, lanes in enumerate(sides)
        ]

    @pl.loop(0, total)
    def _(q):
        for copy in load(q):
            copy.start()

    odd = place[0] % 2
    strips = [
        pltpu.make_async_copy(src, dst.at[slot], strip_sem.at[i])
        for i, (src, dst, slot) in enumerate(
            ((sent_near, mine, 1 - odd), (sent_far, mine, odd), (got_near, halo, 1 - odd), (got_far, halo, odd))
        )
    ]
    for copy in strips:
        copy.start()
    planes = fields * levels
    rates = [pltpu.make_async_copy(hz_any, hz, rate_sem.at[0]), pltpu.make_async_copy(vt_any, vt, rate_sem.at[1])]
    for copy in rates:
        copy.start()
    for copy in rates:
        copy.wait()

    for p in range(planes):
        hcol[p : p + 1, :] = jnp.full((1, half), hz[p // levels, p % levels], jnp.float32)

    for copy in strips:
        copy.wait()
    mine_first, mine_last, before, after = mine.at[0], mine.at[1], halo.at[0], halo.at[1]
    for j in range(4):
        aux[j : j + 1, :] = jnp.full((1, width), (hz[0, 0], hz[0, 1], vt[0], vt[0])[j], jnp.float32)
    aux[4:5, :] = before[1, planes : planes + 1, :]
    aux[5:6, :] = after[0, planes : planes + 1, :]

    level = row_ids(levels, width)
    for side, (x2, x1, x0, m) in enumerate(
        (
            (before.at[0], before.at[1], mine_first.at[0], before[1, planes : planes + 1, :]),
            (after.at[1], after.at[0], mine_last.at[1], after[0, planes : planes + 1, :]),
        )
    ):
        for f in range(fields):
            at = pl.ds(f * levels, levels)
            x = x1[at, :]
            lap = x2[at, :] + x0[at, :] + beside(x)
            below = jnp.where(level == 0, x, pltpu.roll(x, 1, 0))
            above = jnp.where(level == levels - 1, x, pltpu.roll(x, levels - 1, 0))
            h = jnp.concatenate([hcol[at, :]] * 2, 1)
            v = vt[f]
            new = x * (1.0 - 4.0 * h - 2.0 * v) + h * lap + v * (above + below)
            edge[side, at, :] = new * m

    row = row_ids(8, width)
    top, bottom = row == 0, row == 7
    nrow = rows // 8

    def spread(ref, f, l, r):
        return jnp.concatenate([ref[k, f, l, pl.ds(r, 8, stride=nrow), :] for k in range(2)], 1)

    def packed(ref, f, l, r):
        return ref[f, l, pl.ds(8 * r, 8), :]

    for k, lanes in enumerate(sides):
        split[k] = mask[:, lanes]
        for r in range(nrow):
            wet[pl.ds(8 * r, 8), lanes] = split[k, pl.ds(r, 8, stride=nrow), :]

    def substep(get, src, f, l, ahead, behind):
        h, v = hz[f, l], vt[f]
        c0 = 1.0 - 4.0 * h - 2.0 * v
        lo, hi = jnp.maximum(l - 1, 0), jnp.minimum(l + 1, levels - 1)
        p = f * levels + l
        x = [get(src, f, l, r) for r in range(nrow)]
        above = jnp.where(top, jnp.broadcast_to(ahead[pl.ds(p, 1), :], (8, width)), pltpu.roll(x[-1], 1, 0))
        under = jnp.where(bottom, jnp.broadcast_to(behind[pl.ds(p, 1), :], (8, width)), pltpu.roll(x[0], 7, 0))
        for r in range(nrow):
            near = (x[r - 1] if r else above) + (x[r + 1] if r < nrow - 1 else under)
            vert = get(src, f, lo, r) + get(src, f, hi, r)
            new = x[r] * c0 + h * (near + beside(x[r])) + v * vert
            yield r, new * wet[pl.ds(8 * r, 8), :]

    def first(f, l):
        for r, new in substep(spread, raw, f, l, before.at[1], after.at[0]):
            s1[f, l, pl.ds(8 * r, 8), :] = new

    def second(f, l):
        for r, new in substep(packed, s1, f, l, edge.at[0], edge.at[1]):
            for k, lanes in enumerate(sides):
                res[k, f, l, pl.ds(r, 8, stride=nrow), :] = new[:, k * half : (k + 1) * half]

    for copy in load(0):
        copy.wait()

    @pl.loop(0, total + 1)
    def _(q):
        @pl.when(q < total - 1)
        def _():
            for copy in load(q + 1):
                copy.wait()

        @pl.when(q < total)
        def _():
            @pl.loop(0, CHUNK, unroll=UNROLL)
            def _(i):
                first(q // per, (q % per) * CHUNK + i)

        @pl.when(q > 0)
        def _():
            @pl.loop(0, CHUNK, unroll=UNROLL)
            def _(i):
                second((q - 1) // per, ((q - 1) % per) * CHUNK + i)

            for copy in store(q - 1):
                copy.start()

        @pl.when(q == 1)
        def _():
            for k, lanes in enumerate(sides):
                base[:, :, lanes] = res[k, 0, 0:3]

    @pl.loop(0, total)
    def _(q):
        for copy in store(q):
            copy.wait()


def mix(place, fields, hz, vt, sent_near, sent_far, got_near, got_far, mask):
    nf, levels, rows, width = fields.shape
    planes = nf * levels
    vmem = pl.BlockSpec(memory_space=pltpu.VMEM)
    smem = pl.BlockSpec(memory_space=pltpu.SMEM)
    anyw = pl.BlockSpec(memory_space=pl.ANY)
    hbm = pl.BlockSpec(memory_space=pltpu.HBM)
    total = nf * levels // CHUNK
    halved = (2, nf, levels, rows, width // 2)
    return pl.pallas_call(
        mix_kernel,
        out_shape=(
            jax.ShapeDtypeStruct(fields.shape, jnp.float32),
            jax.ShapeDtypeStruct((3, rows, width), jnp.float32),
            jax.ShapeDtypeStruct((8, width), jnp.float32),
        ),
        in_specs=[smem, hbm, hbm, hbm, anyw, anyw, anyw, anyw, vmem],
        out_specs=(hbm, vmem, vmem),
        scratch_shapes=[
            pltpu.VMEM((2, 2, planes + 8, width), jnp.float32),
            pltpu.VMEM((2, 2, planes + 8, width), jnp.float32),
            pltpu.SemaphoreType.DMA((4,)),
            pltpu.SMEM((nf, levels), jnp.float32),
            pltpu.SMEM((nf,), jnp.float32),
            pltpu.VMEM((planes, width // 2), jnp.float32),
            pltpu.VMEM(halved, jnp.float32),
            pltpu.VMEM(fields.shape, jnp.float32),
            pltpu.VMEM(halved, jnp.float32),
            pltpu.VMEM((2, planes, width), jnp.float32),
            pltpu.VMEM((2, rows, width // 2), jnp.float32),
            pltpu.VMEM((rows, width), jnp.float32),
            pltpu.SemaphoreType.DMA((2,)),
            pltpu.SemaphoreType.DMA((total, 2)),
            pltpu.SemaphoreType.DMA((total, 2)),
        ],
        compiler_params=pltpu.CompilerParams(vmem_limit_bytes=46 * MIB),
        cost_estimate=pl.CostEstimate(flops=26 * fields.size, bytes_accessed=8 * fields.size, transcendentals=0),
        name="mix",
    )(place, hz, vt, fields, sent_near, sent_far, got_near, got_far, mask)


def prep_kernel(atmos, state, coef_hbm, sea_hbm, out, wet, surface, coef, sea, sem):
    rows, width = coef.shape
    half = width // 2
    copies = [
        pltpu.make_async_copy(state.at[0, 0], surface, sem.at[0]),
        pltpu.make_async_copy(coef_hbm, coef, sem.at[1]),
        pltpu.make_async_copy(sea_hbm, sea, sem.at[2]),
    ]
    for copy in copies:
        copy.start()
    for copy in copies:
        copy.wait()
    ocean = sea[...].astype(jnp.float32)
    mine = atmos[0] == 1
    second = jnp.where(mine, coef[...], ocean)
    wet[...] = jnp.where(mine, jnp.ones_like(ocean), ocean)
    for k in range(2):
        lanes = slice(k * half, (k + 1) * half)
        out[pl.ds(2 * k * rows, rows, stride=2), :] = surface[:, lanes]
        out[pl.ds(2 * k * rows + 1, rows, stride=2), :] = second[:, lanes]


def prep(atmos, fields, coef, sea):
    smem = pl.BlockSpec(memory_space=pltpu.SMEM)
    vmem = pl.BlockSpec(memory_space=pltpu.VMEM)
    hbm = pl.BlockSpec(memory_space=pltpu.HBM)
    rows, width = coef.shape
    return pl.pallas_call(
        prep_kernel,
        out_shape=(
            jax.ShapeDtypeStruct((4 * rows, width // 2), jnp.float32),
            jax.ShapeDtypeStruct((rows, width), jnp.float32),
        ),
        in_specs=[smem, hbm, hbm, hbm],
        out_specs=(vmem, vmem),
        scratch_shapes=[
            pltpu.VMEM((rows, width), jnp.float32),
            pltpu.VMEM((rows, width), jnp.float32),
            pltpu.VMEM((rows, width), jnp.int32),
            pltpu.SemaphoreType.DMA((3,)),
        ],
        compiler_params=pltpu.CompilerParams(vmem_limit_bytes=60 * MIB),
        cost_estimate=pl.CostEstimate(flops=3 * coef.size, bytes_accessed=24 * coef.size, transcendentals=0),
        name="prep",
    )(atmos, fields, coef, sea)


def edge_kernel(place, atmos, state, sea_any, near, far, stage, sea, sem):
    nf, levels, rows, width = state.shape
    planes = nf * levels
    copies = [
        pltpu.make_async_copy(state.at[:, :, pl.ds(at, 8), :], stage.at[side], sem.at[side])
        for side, at in enumerate((0, rows - 8))
    ]
    copies.append(pltpu.make_async_copy(sea_any, sea, sem.at[2]))
    for copy in copies:
        copy.start()
    for copy in copies:
        copy.wait()

    def fill(first, last):
        for side, (out, at) in enumerate(((first, 0), (last, 6))):
            for j in range(2):
                for f in range(nf):
                    for g in range(0, levels, 8):
                        p = f * levels + g
                        out[j, p : p + 8, :] = stage[side, f, g : g + 8, at + j, :]
                row = side * (rows - 2) + j
                wet = jnp.where(atmos[0] == 1, 1.0, sea[row : row + 1, :].astype(jnp.float32))
                out[j, planes : planes + 8, :] = jnp.broadcast_to(wet, (8, width))

    even = place[0] % 2 == 0

    @pl.when(even)
    def _():
        fill(far, near)

    @pl.when(jnp.logical_not(even))
    def _():
        fill(near, far)


def edges(place, atmos, fields, sea):
    smem = pl.BlockSpec(memory_space=pltpu.SMEM)
    vmem = pl.BlockSpec(memory_space=pltpu.VMEM)
    anyw = pl.BlockSpec(memory_space=pl.ANY)
    hbm = pl.BlockSpec(memory_space=pltpu.HBM)
    nf, levels, _, width = fields.shape
    shape = jax.ShapeDtypeStruct((2, nf * levels + 8, width), jnp.float32)
    return pl.pallas_call(
        edge_kernel,
        out_shape=(shape, shape),
        in_specs=[smem, smem, hbm, anyw],
        out_specs=(vmem, vmem),
        scratch_shapes=[
            pltpu.VMEM((2, nf, levels, 8, width), jnp.float32),
            pltpu.VMEM(sea.shape, jnp.int32),
            pltpu.SemaphoreType.DMA((3,)),
        ],
        compiler_params=pltpu.CompilerParams(vmem_limit_bytes=46 * MIB),
        cost_estimate=pl.CostEstimate(flops=0, bytes_accessed=4 * MIB, transcendentals=0),
        name="edges",
    )(place, atmos, fields, sea)


def flux_kernel(partner, place, got, back, theirs, mine, other):
    tiles = got.shape[0] // 4
    for t in range(tiles):
        theirs[2 * t : 2 * t + 2, :] = got[pl.ds(2 * tiles + 2 * partner[t], 2), :]
    odd, even = pl.ds(1, tiles, stride=2), pl.ds(0, tiles, stride=2)
    flux = got[odd, :] * (got[even, :] - theirs[even, :]) * theirs[odd, :]
    mine[...] = flux
    for t in range(tiles):
        other[pl.ds(partner[t], 1), :] = mine[t : t + 1, :]
    turned = other[...]
    shift = jnp.where(place[0] < 2, tiles - 1, 1)
    back[even, :] = flux
    back[odd, :] = pltpu.roll(flux, shift, 0)
    back[pl.ds(2 * tiles, tiles, stride=2), :] = turned
    back[pl.ds(2 * tiles + 1, tiles, stride=2), :] = pltpu.roll(turned, shift, 0)


def flux_pieces(partner, place, got):
    vmem = pl.BlockSpec(memory_space=pltpu.VMEM)
    smem = pl.BlockSpec(memory_space=pltpu.SMEM)
    tiles, half = got.shape[0] // 4, got.shape[1]
    return pl.pallas_call(
        flux_kernel,
        out_shape=jax.ShapeDtypeStruct(got.shape, jnp.float32),
        in_specs=[smem, smem, vmem],
        out_specs=vmem,
        scratch_shapes=[
            pltpu.VMEM((2 * tiles, half), jnp.float32),
            pltpu.VMEM((tiles, half), jnp.float32),
            pltpu.VMEM((tiles, half), jnp.float32),
        ],
        compiler_params=pltpu.CompilerParams(vmem_limit_bytes=2 * MIB),
        cost_estimate=pl.CostEstimate(flops=10**12, bytes_accessed=8 * got.size, transcendentals=0),
        name="flux",
    )(partner, place, got)


def add_kernel(sign, base, back, mask, aux, whole, out, ext, three, sem):
    del whole
    rows, width = mask.shape
    half = width // 2
    s = sign[0]
    h0, h1, v = (aux[j : j + 1, :] for j in range(3))
    zero_pad = jnp.zeros((8, width), jnp.float32)
    ext[0:8, :] = zero_pad
    ext[8 + rows : 16 + rows, :] = zero_pad
    for k in range(2):
        lanes = pl.ds(k * half, half)
        at = 2 * k * rows
        ext[8 : 8 + rows, lanes] = back[pl.ds(at, rows, stride=2), :] * s
        for j in range(2):
            ext[6 + j : 7 + j, lanes] = back[pl.ds(at + 2 * (rows - 2 + j) + 1, 1), :] * s
            ext[8 + rows + j : 9 + rows + j, lanes] = back[pl.ds(at + 2 * j + 1, 1), :] * s

    total = rows + 16
    m = jnp.concatenate(
        [jnp.broadcast_to(aux[4:5, :], (8, width)), mask[...], jnp.broadcast_to(aux[5:6, :], (8, width))], 0
    )

    def lateral(x):
        return pltpu.roll(x, 1, 0) + pltpu.roll(x, total - 1, 0) + beside(x)

    d = ext[...]
    one0 = m * ((1.0 - 4.0 * h0 - v) * d + h0 * lateral(d))
    one1 = m * (v * d)
    two0 = (1.0 - 4.0 * h0 - v) * one0 + h0 * lateral(one0) + v * one1
    two1 = (1.0 - 4.0 * h1 - 2.0 * v) * one1 + h1 * lateral(one1) + v * one0
    two2 = v * one1
    for level, two in enumerate((two0, two1, two2)):
        three[level] = base[level] + (m * two)[8 : 8 + rows]
    copy = pltpu.make_async_copy(three, out.at[0, pl.ds(0, 3)], sem)
    copy.start()
    copy.wait()


def add_flux(sign, base, back, mask, aux, whole):
    vmem = pl.BlockSpec(memory_space=pltpu.VMEM)
    smem = pl.BlockSpec(memory_space=pltpu.SMEM)
    hbm = pl.BlockSpec(memory_space=pltpu.HBM)
    rows, width = mask.shape
    return pl.pallas_call(
        add_kernel,
        out_shape=jax.ShapeDtypeStruct(whole.shape, jnp.float32),
        in_specs=[smem, vmem, vmem, vmem, vmem, hbm],
        out_specs=hbm,
        scratch_shapes=[pltpu.VMEM((rows + 16, width), jnp.float32), pltpu.VMEM(base.shape, jnp.float32), pltpu.SemaphoreType.DMA],
        input_output_aliases={5: 0},
        compiler_params=pltpu.CompilerParams(vmem_limit_bytes=2 * MIB),
        cost_estimate=pl.CostEstimate(flops=30 * mask.size, bytes_accessed=32 * mask.size, transcendentals=0),
        name="add",
    )(sign, base, back, mask, aux, whole)


def per_device(state, horiz_rate, vert_rate, sea_mask, exchange_coef, partner):
    is_atmos = lax.axis_index("comp") == 0
    ntile = lax.axis_size("tile")
    fields, hz, vt = state[0], horiz_rate[0], vert_rate[0]
    atmos = is_atmos.astype(jnp.int32).reshape(1)
    outgoing, scale = prep(atmos, fields, exchange_coef, sea_mask)
    got = lax.all_to_all(outgoing, BOTH, 0, 0, tiled=True)
    place = lax.axis_index("tile").astype(jnp.int32).reshape(1)
    pieces = flux_pieces(partner, place, got)
    back = lax.all_to_all(pieces, BOTH, 0, 0, tiled=True)

    sent_near, sent_far = edges(place, atmos, fields, sea_mask)
    got_near = lax.ppermute(sent_near, "tile", [(i, i ^ 1) for i in range(ntile)])
    got_far = lax.ppermute(sent_far, "tile", [(i, (i + 2 * (i % 2) - 1) % ntile) for i in range(ntile)])
    whole, base, aux = mix(place, fields, hz, vt, sent_near, sent_far, got_near, got_far, scale)
    sign = jnp.where(is_atmos, -1.0, 1.0).astype(jnp.float32).reshape(1)
    return add_flux(sign, base, back, scale, aux, whole)[None]


def solution(mesh):
    placed = (
        P("comp", None, None, "tile", None),
        P("comp", None, None),
        P("comp", None),
        P("tile", None),
        P("tile", None),
        P(),
    )
    return jax.shard_map(
        per_device,
        mesh=mesh,
        in_specs=placed,
        out_specs=P("comp", None, None, "tile", None),
        check_vma=False,
    )
```

```python
import functools

import jax
import jax.numpy as jnp
from jax import lax
from jax.experimental import pallas as pl
from jax.experimental.pallas import tpu as pltpu
from jax.sharding import PartitionSpec as P

BOTH = ("comp", "tile")
CHUNK = 8
BLOCK = 16
MIB = 1 << 20


def row_ids(rows, width):
    return lax.broadcasted_iota(jnp.int32, (rows, width), 0)


def beside(x):
    half = x.shape[-1] // 2
    a, b = x[:, :half], x[:, half:]
    lane = lax.broadcasted_iota(jnp.int32, a.shape, 1)
    first, last = lane == 0, lane == half - 1
    ra, rb = pltpu.roll(a, 1, 1), pltpu.roll(b, 1, 1)
    la, lb = pltpu.roll(a, half - 1, 1), pltpu.roll(b, half - 1, 1)
    left = jnp.where(first, rb, ra) + jnp.where(last, lb, la)
    right = jnp.where(first, ra, rb) + jnp.where(last, la, lb)
    return jnp.concatenate([left, right], 1)


def mix_kernel(
    place, hz_any, vt_any, state, sent_near, sent_far, got_near, got_far, mask, out, base, aux,
    mine, halo, strip_sem, hz, vt, hcol, raw, s0, s1, res, edge, split, wet, rate_sem, in_sem, out_sem,
):
    fields, levels, rows, width = state.shape
    per = levels // CHUNK
    total = fields * per
    half = width // 2
    sides = [pl.ds(k * half, half) for k in range(2)]

    def load(q):
        f, c = q // per, q % per
        where = (f, pl.ds(c * CHUNK, CHUNK))
        return [
            pltpu.make_async_copy(state.at[(*where, slice(None), lanes)], raw.at[(k, *where)], in_sem.at[q, k])
            for k, lanes in enumerate(sides)
        ]

    def store(q):
        f, c = q // per, q % per
        where = (f, pl.ds(c * CHUNK, CHUNK))
        return [
            pltpu.make_async_copy(res.at[(k, *where)], out.at[(*where, slice(None), lanes)], out_sem.at[q, k])
            for k, lanes in enumerate(sides)
        ]

    odd = place[0] % 2
    strips = [
        pltpu.make_async_copy(src, dst.at[slot], strip_sem.at[i])
        for i, (src, dst, slot) in enumerate(
            ((sent_near, mine, 1 - odd), (sent_far, mine, odd), (got_near, halo, 1 - odd), (got_far, halo, odd))
        )
    ]
    for copy in strips:
        copy.start()
    planes = fields * levels
    rates = [pltpu.make_async_copy(hz_any, hz, rate_sem.at[0]), pltpu.make_async_copy(vt_any, vt, rate_sem.at[1])]
    for copy in rates:
        copy.start()

    @pl.loop(0, total)
    def _(q):
        for copy in load(q):
            copy.start()

    for copy in rates:
        copy.wait()

    for p in range(planes):
        hcol[p : p + 1, :] = jnp.full((1, half), hz[p // levels, p % levels], jnp.float32)

    for copy in strips:
        copy.wait()
    mine_first, mine_last, before, after = mine.at[0], mine.at[1], halo.at[0], halo.at[1]
    for j in range(4):
        aux[j : j + 1, :] = jnp.full((1, width), (hz[0, 0], hz[0, 1], vt[0], vt[0])[j], jnp.float32)
    aux[4:5, :] = before[1, planes : planes + 1, :]
    aux[5:6, :] = after[0, planes : planes + 1, :]

    level = row_ids(levels, width)
    for side, (x2, x1, x0, m) in enumerate(
        (
            (before.at[0], before.at[1], mine_first.at[0], before[1, planes : planes + 1, :]),
            (after.at[1], after.at[0], mine_last.at[1], after[0, planes : planes + 1, :]),
        )
    ):
        for f in range(fields):
            at = pl.ds(f * levels, levels)
            x = x1[at, :]
            lap = x2[at, :] + x0[at, :] + beside(x)
            below = jnp.where(level == 0, x, pltpu.roll(x, 1, 0))
            above = jnp.where(level == levels - 1, x, pltpu.roll(x, levels - 1, 0))
            h = jnp.concatenate([hcol[at, :]] * 2, 1)
            v = vt[f]
            new = x * (1.0 - 4.0 * h - 2.0 * v) + h * lap + v * (above + below)
            edge[side, at, :] = new * m

    row = row_ids(8, width)
    top, bottom = row == 0, row == 7
    nrow = rows // 8

    def spread(ref, f, l, r):
        return jnp.concatenate([ref[k, f, l, pl.ds(r, 8, stride=nrow), :] for k in range(2)], 1)

    def packed(ref, f, l, r):
        return ref[f, l, pl.ds(8 * r, 8), :]

    for k, lanes in enumerate(sides):
        split[k] = mask[:, lanes]
        for r in range(nrow):
            wet[pl.ds(8 * r, 8), lanes] = split[k, pl.ds(r, 8, stride=nrow), :]

    def pack(f, l):
        for r in range(nrow):
            s0[f, l, pl.ds(8 * r, 8), :] = spread(raw, f, l, r)

    def substep(src, f, base, i, ahead, behind):
        l = base + i
        h, v = hz[f, l], vt[f]
        c0 = 1.0 - 4.0 * h - 2.0 * v
        lo = l - 1 if i else jnp.maximum(l - 1, 0)
        hi = l + 1 if i < BLOCK - 1 else jnp.minimum(l + 1, levels - 1)
        p = f * levels + l
        x = [src[f, l, pl.ds(8 * r, 8), :] for r in range(nrow)]
        above = jnp.where(top, jnp.broadcast_to(ahead[pl.ds(p, 1), :], (8, width)), pltpu.roll(x[-1], 1, 0))
        under = jnp.where(bottom, jnp.broadcast_to(behind[pl.ds(p, 1), :], (8, width)), pltpu.roll(x[0], 7, 0))
        for r in range(nrow):
            at = pl.ds(8 * r, 8)
            near = (x[r - 1] if r else above) + (x[r + 1] if r < nrow - 1 else under)
            vert = src[f, lo, at, :] + src[f, hi, at, :]
            new = x[r] * c0 + h * (near + beside(x[r])) + v * vert
            yield r, new * wet[at, :]

    def first(f, base, i):
        pack(f, base + i + 1 if i < BLOCK - 1 else jnp.minimum(base + i + 1, levels - 1))
        for r, new in substep(s0, f, base, i, before.at[1], after.at[0]):
            s1[f, base + i, pl.ds(8 * r, 8), :] = new

    def second(f, base, i):
        for r, new in substep(s1, f, base, i, edge.at[0], edge.at[1]):
            for k in range(2):
                res[k, f, base + i, pl.ds(r, 8, stride=nrow), :] = new[:, k * half : (k + 1) * half]

    blocks, step = fields * levels // BLOCK, BLOCK // CHUNK

    for copy in load(0):
        copy.wait()

    @pl.loop(0, blocks + 1)
    def _(q):
        for j in range(1, step + 1):
            @pl.when(q * step + j < total)
            def _(j=j):
                for copy in load(q * step + j):
                    copy.wait()

        @pl.when(q * BLOCK % levels == 0)
        def _():
            pack(jnp.minimum(q * BLOCK // levels, fields - 1), 0)

        @pl.when(q < blocks)
        def _():
            f, l = q * BLOCK // levels, q * BLOCK % levels
            for i in range(BLOCK):
                first(f, l, i)

        @pl.when(q > 0)
        def _():
            f, l = (q - 1) * BLOCK // levels, (q - 1) * BLOCK % levels
            for i in range(BLOCK):
                second(f, l, i)

            for j in range(step):
                for copy in store((q - 1) * step + j):
                    copy.start()

        @pl.when(q == 1)
        def _():
            for k, lanes in enumerate(sides):
                base[:, :, lanes] = res[k, 0, 0:3]

    @pl.loop(0, total)
    def _(q):
        for copy in store(q):
            copy.wait()


def mix(place, fields, hz, vt, sent_near, sent_far, got_near, got_far, mask):
    nf, levels, rows, width = fields.shape
    planes = nf * levels
    vmem = pl.BlockSpec(memory_space=pltpu.VMEM)
    smem = pl.BlockSpec(memory_space=pltpu.SMEM)
    hbm = pl.BlockSpec(memory_space=pltpu.HBM)
    total = nf * levels // CHUNK
    halved = (2, nf, levels, rows, width // 2)
    return pl.pallas_call(
        mix_kernel,
        out_shape=(
            jax.ShapeDtypeStruct(fields.shape, jnp.float32),
            jax.ShapeDtypeStruct((3, rows, width), jnp.float32),
            jax.ShapeDtypeStruct((8, width), jnp.float32),
        ),
        in_specs=[smem, hbm, hbm, hbm, vmem, vmem, vmem, vmem, vmem],
        out_specs=(hbm, vmem, vmem),
        scratch_shapes=[
            pltpu.VMEM((2, 2, planes + 8, width), jnp.float32),
            pltpu.VMEM((2, 2, planes + 8, width), jnp.float32),
            pltpu.SemaphoreType.DMA((4,)),
            pltpu.SMEM((nf, levels), jnp.float32),
            pltpu.SMEM((nf,), jnp.float32),
            pltpu.VMEM((planes, width // 2), jnp.float32),
            pltpu.VMEM(halved, jnp.float32),
            pltpu.VMEM(fields.shape, jnp.float32),
            pltpu.VMEM(fields.shape, jnp.float32),
            pltpu.VMEM(halved, jnp.float32),
            pltpu.VMEM((2, planes, width), jnp.float32),
            pltpu.VMEM((2, rows, width // 2), jnp.float32),
            pltpu.VMEM((rows, width), jnp.float32),
            pltpu.SemaphoreType.DMA((2,)),
            pltpu.SemaphoreType.DMA((total, 2)),
            pltpu.SemaphoreType.DMA((total, 2)),
        ],
        compiler_params=pltpu.CompilerParams(vmem_limit_bytes=46 * MIB),
        cost_estimate=pl.CostEstimate(flops=26 * fields.size, bytes_accessed=8 * fields.size, transcendentals=0),
        name="mix",
    )(place, hz, vt, fields, sent_near, sent_far, got_near, got_far, mask)


def prep_kernel(atmos, state, coef_hbm, sea_hbm, out, wet, surface, coef, sea, sem):
    rows, width = coef.shape
    half = width // 2
    copies = [
        pltpu.make_async_copy(state.at[0, 0], surface, sem.at[0]),
        pltpu.make_async_copy(coef_hbm, coef, sem.at[1]),
        pltpu.make_async_copy(sea_hbm, sea, sem.at[2]),
    ]
    for copy in copies:
        copy.start()
    for copy in copies:
        copy.wait()
    ocean = sea[...].astype(jnp.float32)
    mine = atmos[0] == 1
    second = jnp.where(mine, coef[...], ocean)
    wet[...] = jnp.where(mine, jnp.ones_like(ocean), ocean)
    for k in range(2):
        lanes = slice(k * half, (k + 1) * half)
        out[pl.ds(2 * k * rows, rows, stride=2), :] = surface[:, lanes]
        out[pl.ds(2 * k * rows + 1, rows, stride=2), :] = second[:, lanes]


def prep(atmos, fields, coef, sea):
    smem = pl.BlockSpec(memory_space=pltpu.SMEM)
    vmem = pl.BlockSpec(memory_space=pltpu.VMEM)
    hbm = pl.BlockSpec(memory_space=pltpu.HBM)
    rows, width = coef.shape
    return pl.pallas_call(
        prep_kernel,
        out_shape=(
            jax.ShapeDtypeStruct((4 * rows, width // 2), jnp.float32),
            jax.ShapeDtypeStruct((rows, width), jnp.float32),
        ),
        in_specs=[smem, hbm, hbm, hbm],
        out_specs=(vmem, vmem),
        scratch_shapes=[
            pltpu.VMEM((rows, width), jnp.float32),
            pltpu.VMEM((rows, width), jnp.float32),
            pltpu.VMEM((rows, width), jnp.int32),
            pltpu.SemaphoreType.DMA((3,)),
        ],
        compiler_params=pltpu.CompilerParams(vmem_limit_bytes=60 * MIB),
        cost_estimate=pl.CostEstimate(flops=3 * coef.size, bytes_accessed=24 * coef.size, transcendentals=0),
        name="prep",
    )(atmos, fields, coef, sea)


def edge_kernel(place, atmos, state, sea_any, near, far, stage, sea, sem):
    nf, levels, rows, width = state.shape
    planes = nf * levels
    copies = [
        pltpu.make_async_copy(state.at[:, :, pl.ds(at, 8), :], stage.at[side], sem.at[side])
        for side, at in enumerate((0, rows - 8))
    ]
    copies.append(pltpu.make_async_copy(sea_any, sea, sem.at[2]))
    for copy in copies:
        copy.start()
    for copy in copies:
        copy.wait()

    def fill(first, last):
        for side, (out, at) in enumerate(((first, 0), (last, 6))):
            for j in range(2):
                for f in range(nf):
                    for g in range(0, levels, 8):
                        p = f * levels + g
                        out[j, p : p + 8, :] = stage[side, f, g : g + 8, at + j, :]
                row = side * (rows - 2) + j
                wet = jnp.where(atmos[0] == 1, 1.0, sea[row : row + 1, :].astype(jnp.float32))
                out[j, planes : planes + 8, :] = jnp.broadcast_to(wet, (8, width))

    even = place[0] % 2 == 0

    @pl.when(even)
    def _():
        fill(far, near)

    @pl.when(jnp.logical_not(even))
    def _():
        fill(near, far)


def edges(place, atmos, fields, sea):
    smem = pl.BlockSpec(memory_space=pltpu.SMEM)
    vmem = pl.BlockSpec(memory_space=pltpu.VMEM)
    anyw = pl.BlockSpec(memory_space=pl.ANY)
    hbm = pl.BlockSpec(memory_space=pltpu.HBM)
    nf, levels, _, width = fields.shape
    shape = jax.ShapeDtypeStruct((2, nf * levels + 8, width), jnp.float32)
    return pl.pallas_call(
        edge_kernel,
        out_shape=(shape, shape),
        in_specs=[smem, smem, hbm, anyw],
        out_specs=(vmem, vmem),
        scratch_shapes=[
            pltpu.VMEM((2, nf, levels, 8, width), jnp.float32),
            pltpu.VMEM(sea.shape, jnp.int32),
            pltpu.SemaphoreType.DMA((3,)),
        ],
        compiler_params=pltpu.CompilerParams(vmem_limit_bytes=46 * MIB),
        cost_estimate=pl.CostEstimate(flops=0, bytes_accessed=4 * MIB, transcendentals=0),
        name="edges",
    )(place, atmos, fields, sea)


def flux_kernel(partner, place, got, back, theirs, mine, other):
    tiles = got.shape[0] // 4
    for t in range(tiles):
        theirs[2 * t : 2 * t + 2, :] = got[pl.ds(2 * tiles + 2 * partner[t], 2), :]
    odd, even = pl.ds(1, tiles, stride=2), pl.ds(0, tiles, stride=2)
    flux = got[odd, :] * (got[even, :] - theirs[even, :]) * theirs[odd, :]
    mine[...] = flux
    for t in range(tiles):
        other[pl.ds(partner[t], 1), :] = mine[t : t + 1, :]
    turned = other[...]
    shift = jnp.where(place[0] < 2, tiles - 1, 1)
    back[even, :] = flux
    back[odd, :] = pltpu.roll(flux, shift, 0)
    back[pl.ds(2 * tiles, tiles, stride=2), :] = turned
    back[pl.ds(2 * tiles + 1, tiles, stride=2), :] = pltpu.roll(turned, shift, 0)


def flux_pieces(partner, place, got):
    vmem = pl.BlockSpec(memory_space=pltpu.VMEM)
    smem = pl.BlockSpec(memory_space=pltpu.SMEM)
    tiles, half = got.shape[0] // 4, got.shape[1]
    return pl.pallas_call(
        flux_kernel,
        out_shape=jax.ShapeDtypeStruct(got.shape, jnp.float32),
        in_specs=[smem, smem, vmem],
        out_specs=vmem,
        scratch_shapes=[
            pltpu.VMEM((2 * tiles, half), jnp.float32),
            pltpu.VMEM((tiles, half), jnp.float32),
            pltpu.VMEM((tiles, half), jnp.float32),
        ],
        compiler_params=pltpu.CompilerParams(vmem_limit_bytes=2 * MIB),
        cost_estimate=pl.CostEstimate(flops=10**12, bytes_accessed=8 * got.size, transcendentals=0),
        name="flux",
    )(partner, place, got)


def add_kernel(sign, base, back, mask, aux, whole, out, ext, three, sem):
    del whole
    rows, width = mask.shape
    half = width // 2
    s = sign[0]
    h0, h1, v = (aux[j : j + 1, :] for j in range(3))
    zero_pad = jnp.zeros((8, width), jnp.float32)
    ext[0:8, :] = zero_pad
    ext[8 + rows : 16 + rows, :] = zero_pad
    for k in range(2):
        lanes = pl.ds(k * half, half)
        at = 2 * k * rows
        ext[8 : 8 + rows, lanes] = back[pl.ds(at, rows, stride=2), :] * s
        for j in range(2):
            ext[6 + j : 7 + j, lanes] = back[pl.ds(at + 2 * (rows - 2 + j) + 1, 1), :] * s
            ext[8 + rows + j : 9 + rows + j, lanes] = back[pl.ds(at + 2 * j + 1, 1), :] * s

    total = rows + 16
    m = jnp.concatenate(
        [jnp.broadcast_to(aux[4:5, :], (8, width)), mask[...], jnp.broadcast_to(aux[5:6, :], (8, width))], 0
    )

    def lateral(x):
        return pltpu.roll(x, 1, 0) + pltpu.roll(x, total - 1, 0) + beside(x)

    d = ext[...]
    one0 = m * ((1.0 - 4.0 * h0 - v) * d + h0 * lateral(d))
    one1 = m * (v * d)
    two0 = (1.0 - 4.0 * h0 - v) * one0 + h0 * lateral(one0) + v * one1
    two1 = (1.0 - 4.0 * h1 - 2.0 * v) * one1 + h1 * lateral(one1) + v * one0
    two2 = v * one1
    for level, two in enumerate((two0, two1, two2)):
        three[level] = base[level] + (m * two)[8 : 8 + rows]
    copy = pltpu.make_async_copy(three, out.at[0, pl.ds(0, 3)], sem)
    copy.start()
    copy.wait()


def add_flux(sign, base, back, mask, aux, whole):
    vmem = pl.BlockSpec(memory_space=pltpu.VMEM)
    smem = pl.BlockSpec(memory_space=pltpu.SMEM)
    hbm = pl.BlockSpec(memory_space=pltpu.HBM)
    rows, width = mask.shape
    return pl.pallas_call(
        add_kernel,
        out_shape=jax.ShapeDtypeStruct(whole.shape, jnp.float32),
        in_specs=[smem, vmem, vmem, vmem, vmem, hbm],
        out_specs=hbm,
        scratch_shapes=[pltpu.VMEM((rows + 16, width), jnp.float32), pltpu.VMEM(base.shape, jnp.float32), pltpu.SemaphoreType.DMA],
        input_output_aliases={5: 0},
        compiler_params=pltpu.CompilerParams(vmem_limit_bytes=2 * MIB),
        cost_estimate=pl.CostEstimate(flops=30 * mask.size, bytes_accessed=32 * mask.size, transcendentals=0),
        name="add",
    )(sign, base, back, mask, aux, whole)


def per_device(state, horiz_rate, vert_rate, sea_mask, exchange_coef, partner):
    is_atmos = lax.axis_index("comp") == 0
    ntile = lax.axis_size("tile")
    fields, hz, vt = state[0], horiz_rate[0], vert_rate[0]
    atmos = is_atmos.astype(jnp.int32).reshape(1)
    outgoing, scale = prep(atmos, fields, exchange_coef, sea_mask)
    got = lax.all_to_all(outgoing, BOTH, 0, 0, tiled=True)
    place = lax.axis_index("tile").astype(jnp.int32).reshape(1)
    pieces = flux_pieces(partner, place, got)
    back = lax.all_to_all(pieces, BOTH, 0, 0, tiled=True)

    sent_near, sent_far = edges(place, atmos, fields, sea_mask)
    got_near = lax.ppermute(sent_near, "tile", [(i, i ^ 1) for i in range(ntile)])
    got_far = lax.ppermute(sent_far, "tile", [(i, (i + 2 * (i % 2) - 1) % ntile) for i in range(ntile)])
    whole, base, aux = mix(place, fields, hz, vt, sent_near, sent_far, got_near, got_far, scale)
    sign = jnp.where(is_atmos, -1.0, 1.0).astype(jnp.float32).reshape(1)
    return add_flux(sign, base, back, scale, aux, whole)[None]


def solution(mesh):
    placed = (
        P("comp", None, None, "tile", None),
        P("comp", None, None),
        P("comp", None),
        P("tile", None),
        P("tile", None),
        P(),
    )
    return jax.shard_map(
        per_device,
        mesh=mesh,
        in_specs=placed,
        out_specs=P("comp", None, None, "tile", None),
        check_vma=False,
    )
```

```python
import functools

import jax
import jax.numpy as jnp
from jax import lax
from jax.experimental import pallas as pl
from jax.experimental.pallas import tpu as pltpu
from jax.sharding import PartitionSpec as P

BOTH = ("comp", "tile")
CHUNK = 8
BLOCK = 16
MIB = 1 << 20


def row_ids(rows, width):
    return lax.broadcasted_iota(jnp.int32, (rows, width), 0)


def beside(x):
    half = x.shape[-1] // 2
    a, b = x[:, :half], x[:, half:]
    lane = lax.broadcasted_iota(jnp.int32, a.shape, 1)
    first, last = lane == 0, lane == half - 1
    ra, rb = pltpu.roll(a, 1, 1), pltpu.roll(b, 1, 1)
    la, lb = pltpu.roll(a, half - 1, 1), pltpu.roll(b, half - 1, 1)
    left = jnp.where(first, rb, ra) + jnp.where(last, lb, la)
    right = jnp.where(first, ra, rb) + jnp.where(last, la, lb)
    return jnp.concatenate([left, right], 1)


def mix_kernel(
    hz_any, vt_any, state, sent_near, sent_far, got_near, got_far, mask, out, base, aux,
    mine, halo, strip_sem, hz, vt, hcol, raw, s0, s1, res, edge, split, wet, rate_sem, in_sem, out_sem,
):
    planes, rows, width = state.shape
    fields, levels = hz.shape
    total = planes // CHUNK
    half = width // 2
    sides = [pl.ds(k * half, half) for k in range(2)]

    def load(q):
        at = pl.ds(q * CHUNK, CHUNK)
        return [
            pltpu.make_async_copy(state.at[at, :, lanes], raw.at[k, at], in_sem.at[q, k])
            for k, lanes in enumerate(sides)
        ]

    def store(q):
        at = pl.ds(q * CHUNK, CHUNK)
        return [
            pltpu.make_async_copy(res.at[k, at], out.at[at, :, lanes], out_sem.at[q, k])
            for k, lanes in enumerate(sides)
        ]

    odd = lax.axis_index("tile") % 2
    strips = [
        pltpu.make_async_copy(src, dst.at[slot], strip_sem.at[i])
        for i, (src, dst, slot) in enumerate(
            ((sent_near, mine, 1 - odd), (sent_far, mine, odd), (got_near, halo, 1 - odd), (got_far, halo, odd))
        )
    ]
    for copy in strips:
        copy.start()
    rates = [pltpu.make_async_copy(hz_any, hz, rate_sem.at[0]), pltpu.make_async_copy(vt_any, vt, rate_sem.at[1])]
    for copy in rates:
        copy.start()

    @pl.loop(0, total)
    def _(q):
        for copy in load(q):
            copy.start()

    for copy in rates:
        copy.wait()

    for p in range(planes):
        hcol[p : p + 1, :] = jnp.full((1, half), hz[p // levels, p % levels], jnp.float32)

    for copy in strips:
        copy.wait()
    mine_first, mine_last, before, after = mine.at[0], mine.at[1], halo.at[0], halo.at[1]
    for j in range(4):
        aux[j : j + 1, :] = jnp.full((1, width), (hz[0, 0], hz[0, 1], vt[0], vt[0])[j], jnp.float32)
    aux[4:5, :] = before[1, planes : planes + 1, :]
    aux[5:6, :] = after[0, planes : planes + 1, :]

    level = row_ids(levels, width)
    for side, (x2, x1, x0, m) in enumerate(
        (
            (before.at[0], before.at[1], mine_first.at[0], before[1, planes : planes + 1, :]),
            (after.at[1], after.at[0], mine_last.at[1], after[0, planes : planes + 1, :]),
        )
    ):
        for f in range(fields):
            at = pl.ds(f * levels, levels)
            x = x1[at, :]
            lap = x2[at, :] + x0[at, :] + beside(x)
            below = jnp.where(level == 0, x, pltpu.roll(x, 1, 0))
            above = jnp.where(level == levels - 1, x, pltpu.roll(x, levels - 1, 0))
            h = jnp.concatenate([hcol[at, :]] * 2, 1)
            v = vt[f]
            new = x * (1.0 - 4.0 * h - 2.0 * v) + h * lap + v * (above + below)
            edge[side, at, :] = new * m

    row = row_ids(8, width)
    top, bottom = row == 0, row == 7
    nrow = rows // 8

    for k, lanes in enumerate(sides):
        split[k] = mask[:, lanes]
        for r in range(nrow):
            wet[pl.ds(8 * r, 8), lanes] = split[k, pl.ds(r, 8, stride=nrow), :]

    def pack(p):
        for r in range(nrow):
            s0[p, pl.ds(8 * r, 8), :] = jnp.concatenate([raw[k, p, pl.ds(r, 8, stride=nrow), :] for k in range(2)], 1)

    def substep(src, p, lo, hi, ahead, behind):
        f = p // levels
        h, v = hz[f, p % levels], vt[f]
        c0 = 1.0 - 4.0 * h - 2.0 * v
        x = [src[p, pl.ds(8 * r, 8), :] for r in range(nrow)]
        above = jnp.where(top, jnp.broadcast_to(ahead[pl.ds(p, 1), :], (8, width)), pltpu.roll(x[-1], 1, 0))
        under = jnp.where(bottom, jnp.broadcast_to(behind[pl.ds(p, 1), :], (8, width)), pltpu.roll(x[0], 7, 0))
        for r in range(nrow):
            at = pl.ds(8 * r, 8)
            near = (x[r - 1] if r else above) + (x[r + 1] if r < nrow - 1 else under)
            vert = src[lo, at, :] + src[hi, at, :]
            new = x[r] * c0 + h * (near + beside(x[r])) + v * vert
            yield r, new * wet[at, :]

    def first(start, i):
        p = start + i
        pack(p + 1 if i < BLOCK - 1 else jnp.minimum(p + 1, planes - 1))
        lo = p - 1 if i else jnp.where(p % levels == 0, p, p - 1)
        hi = p + 1 if i < BLOCK - 1 else jnp.where(p % levels == levels - 1, p, p + 1)
        for r, new in substep(s0, p, lo, hi, before.at[1], after.at[0]):
            s1[p, pl.ds(8 * r, 8), :] = new

    def second_at(p, lo, hi):
        for r, new in substep(s1, p, lo, hi, edge.at[0], edge.at[1]):
            for k in range(2):
                res[k, p, pl.ds(r, 8, stride=nrow), :] = new[:, k * half : (k + 1) * half]

    def second(start, i):
        p = start + i - 1 if i else jnp.maximum(start - 1, 0)
        lo = p - 1 if i > 1 else jnp.where(p % levels == 0, p, p - 1)
        hi = p + 1 if i else jnp.where(p % levels == levels - 1, p, p + 1)
        second_at(p, lo, hi)

    blocks, step = planes // BLOCK, BLOCK // CHUNK

    def arrive(q):
        for copy in load(q):
            copy.wait()

    def leave(q):
        for copy in store(q):
            copy.start()

    for j in range(step + 1):
        arrive(j)
    pack(0)
    for i in range(BLOCK):
        first(0, i)

    @pl.loop(1, blocks)
    def _(q):
        for j in range(1, step + 1):
            @pl.when(q * step + j < total)
            def _(j=j):
                arrive(q * step + j)

        now = q * BLOCK
        for i in range(BLOCK):
            second(now - BLOCK, i)
        for i in range(BLOCK):
            first(now, i)

        @pl.when(q > 1)
        def _():
            leave((q - 1) * step - 1)

        for j in range(step - 1):
            leave((q - 1) * step + j)

        @pl.when(q == 1)
        def _():
            for k, lanes in enumerate(sides):
                base[:, :, lanes] = res[k, 0:3]

    for i in range(BLOCK):
        second(planes - BLOCK, i)
        if i % CHUNK == 0:
            leave(total - step - 1 + i // CHUNK)
    second_at(planes - 1, planes - 2, planes - 1)
    leave(total - 1)

    @pl.loop(0, total)
    def _(q):
        for copy in store(q):
            copy.wait()


def mix(fields, hz, vt, sent_near, sent_far, got_near, got_far, mask):
    nf, levels, rows, width = fields.shape
    planes = nf * levels
    flat = (planes, rows, width)
    vmem = pl.BlockSpec(memory_space=pltpu.VMEM)
    hbm = pl.BlockSpec(memory_space=pltpu.HBM)
    total = nf * levels // CHUNK
    halved = (2, planes, rows, width // 2)
    whole, base, aux = pl.pallas_call(
        mix_kernel,
        out_shape=(
            jax.ShapeDtypeStruct(flat, jnp.float32),
            jax.ShapeDtypeStruct((3, rows, width), jnp.float32),
            jax.ShapeDtypeStruct((8, width), jnp.float32),
        ),
        in_specs=[hbm, hbm, hbm, vmem, vmem, vmem, vmem, vmem],
        out_specs=(hbm, vmem, vmem),
        scratch_shapes=[
            pltpu.VMEM((2, 2, planes + 8, width), jnp.float32),
            pltpu.VMEM((2, 2, planes + 8, width), jnp.float32),
            pltpu.SemaphoreType.DMA((4,)),
            pltpu.SMEM((nf, levels), jnp.float32),
            pltpu.SMEM((nf,), jnp.float32),
            pltpu.VMEM((planes, width // 2), jnp.float32),
            pltpu.VMEM(halved, jnp.float32),
            pltpu.VMEM(flat, jnp.float32),
            pltpu.VMEM(flat, jnp.float32),
            pltpu.VMEM(halved, jnp.float32),
            pltpu.VMEM((2, planes, width), jnp.float32),
            pltpu.VMEM((2, rows, width // 2), jnp.float32),
            pltpu.VMEM((rows, width), jnp.float32),
            pltpu.SemaphoreType.DMA((2,)),
            pltpu.SemaphoreType.DMA((total, 2)),
            pltpu.SemaphoreType.DMA((total, 2)),
        ],
        compiler_params=pltpu.CompilerParams(vmem_limit_bytes=46 * MIB),
        cost_estimate=pl.CostEstimate(flops=26 * fields.size, bytes_accessed=8 * fields.size, transcendentals=0),
        name="mix",
    )(hz, vt, fields.reshape(flat), sent_near, sent_far, got_near, got_far, mask)
    return whole.reshape(fields.shape), base, aux


def prep_kernel(state, coef_hbm, sea_hbm, out, wet, surface, coef, sea, sem):
    rows, width = coef.shape
    half = width // 2
    copies = [
        pltpu.make_async_copy(state.at[0, 0], surface, sem.at[0]),
        pltpu.make_async_copy(coef_hbm, coef, sem.at[1]),
        pltpu.make_async_copy(sea_hbm, sea, sem.at[2]),
    ]
    for copy in copies:
        copy.start()
    for copy in copies:
        copy.wait()
    ocean = sea[...].astype(jnp.float32)
    mine = lax.axis_index("comp") == 0
    second = jnp.where(mine, coef[...], ocean)
    wet[...] = jnp.where(mine, jnp.ones_like(ocean), ocean)
    for k in range(2):
        lanes = slice(k * half, (k + 1) * half)
        out[pl.ds(2 * k * rows, rows, stride=2), :] = surface[:, lanes]
        out[pl.ds(2 * k * rows + 1, rows, stride=2), :] = second[:, lanes]


def prep(fields, coef, sea):
    vmem = pl.BlockSpec(memory_space=pltpu.VMEM)
    hbm = pl.BlockSpec(memory_space=pltpu.HBM)
    rows, width = coef.shape
    return pl.pallas_call(
        prep_kernel,
        out_shape=(
            jax.ShapeDtypeStruct((4 * rows, width // 2), jnp.float32),
            jax.ShapeDtypeStruct((rows, width), jnp.float32),
        ),
        in_specs=[hbm, hbm, hbm],
        out_specs=(vmem, vmem),
        scratch_shapes=[
            pltpu.VMEM((rows, width), jnp.float32),
            pltpu.VMEM((rows, width), jnp.float32),
            pltpu.VMEM((rows, width), jnp.int32),
            pltpu.SemaphoreType.DMA((3,)),
        ],
        compiler_params=pltpu.CompilerParams(vmem_limit_bytes=60 * MIB),
        cost_estimate=pl.CostEstimate(flops=3 * coef.size, bytes_accessed=24 * coef.size, transcendentals=0),
        name="prep",
    )(fields, coef, sea)


def edge_kernel(state, sea_any, near, far, stage, sea, sem):
    nf, levels, rows, width = state.shape
    planes = nf * levels
    copies = [
        pltpu.make_async_copy(state.at[f, :, pl.ds(at, 8), :], stage.at[side, f], sem.at[side, f])
        for side, at in enumerate((0, rows - 8))
        for f in range(nf)
    ]
    mask_copy = pltpu.make_async_copy(sea_any, sea, sem.at[2, 0])
    mask_copy.start()
    for copy in copies:
        copy.start()
    mask_copy.wait()

    def fill(first, last):
        for side, (out, at) in enumerate(((first, 0), (last, 6))):
            for f in range(nf):
                copies[side * nf + f].wait()
                for j in range(2):
                    for g in range(0, levels, 8):
                        p = f * levels + g
                        out[j, p : p + 8, :] = stage[side, f, g : g + 8, at + j, :]
            for j in range(2):
                row = side * (rows - 2) + j
                wet = jnp.where(lax.axis_index("comp") == 0, 1.0, sea[row : row + 1, :].astype(jnp.float32))
                out[j, planes : planes + 8, :] = jnp.broadcast_to(wet, (8, width))

    even = lax.axis_index("tile") % 2 == 0

    @pl.when(even)
    def _():
        fill(far, near)

    @pl.when(jnp.logical_not(even))
    def _():
        fill(near, far)


def edges(fields, sea):
    vmem = pl.BlockSpec(memory_space=pltpu.VMEM)
    anyw = pl.BlockSpec(memory_space=pl.ANY)
    hbm = pl.BlockSpec(memory_space=pltpu.HBM)
    nf, levels, _, width = fields.shape
    shape = jax.ShapeDtypeStruct((2, nf * levels + 8, width), jnp.float32)
    return pl.pallas_call(
        edge_kernel,
        out_shape=(shape, shape),
        in_specs=[hbm, anyw],
        out_specs=(vmem, vmem),
        scratch_shapes=[
            pltpu.VMEM((2, nf, levels, 8, width), jnp.float32),
            pltpu.VMEM(sea.shape, jnp.int32),
            pltpu.SemaphoreType.DMA((3, nf)),
        ],
        compiler_params=pltpu.CompilerParams(vmem_limit_bytes=46 * MIB),
        cost_estimate=pl.CostEstimate(flops=0, bytes_accessed=4 * MIB, transcendentals=0),
        name="edges",
    )(fields, sea)


def flux_kernel(partner, got, back, theirs, mine, other):
    tiles = got.shape[0] // 4
    for t in range(tiles):
        theirs[2 * t : 2 * t + 2, :] = got[pl.ds(2 * tiles + 2 * partner[t], 2), :]
    odd, even = pl.ds(1, tiles, stride=2), pl.ds(0, tiles, stride=2)
    flux = got[odd, :] * (got[even, :] - theirs[even, :]) * theirs[odd, :]
    mine[...] = flux
    for t in range(tiles):
        other[pl.ds(partner[t], 1), :] = mine[t : t + 1, :]
    turned = other[...]
    shift = jnp.where(lax.axis_index("tile") < 2, tiles - 1, 1)
    back[even, :] = flux
    back[odd, :] = pltpu.roll(flux, shift, 0)
    back[pl.ds(2 * tiles, tiles, stride=2), :] = turned
    back[pl.ds(2 * tiles + 1, tiles, stride=2), :] = pltpu.roll(turned, shift, 0)


def flux_pieces(partner, got):
    vmem = pl.BlockSpec(memory_space=pltpu.VMEM)
    smem = pl.BlockSpec(memory_space=pltpu.SMEM)
    tiles, half = got.shape[0] // 4, got.shape[1]
    return pl.pallas_call(
        flux_kernel,
        out_shape=jax.ShapeDtypeStruct(got.shape, jnp.float32),
        in_specs=[smem, vmem],
        out_specs=vmem,
        scratch_shapes=[
            pltpu.VMEM((2 * tiles, half), jnp.float32),
            pltpu.VMEM((tiles, half), jnp.float32),
            pltpu.VMEM((tiles, half), jnp.float32),
        ],
        compiler_params=pltpu.CompilerParams(vmem_limit_bytes=2 * MIB),
        cost_estimate=pl.CostEstimate(flops=3 * 10**10, bytes_accessed=8 * got.size, transcendentals=0),
        name="flux",
    )(partner, got)


def add_kernel(base, back, mask, aux, whole, out, ext, three, sem):
    del whole
    rows, width = mask.shape
    half = width // 2
    s = jnp.where(lax.axis_index("comp") == 0, -1.0, 1.0).astype(jnp.float32)
    h0, h1, v = (aux[j : j + 1, :] for j in range(3))
    zero_pad = jnp.zeros((8, width), jnp.float32)
    ext[0:8, :] = zero_pad
    ext[8 + rows : 16 + rows, :] = zero_pad
    for k in range(2):
        lanes = pl.ds(k * half, half)
        at = 2 * k * rows
        ext[8 : 8 + rows, lanes] = back[pl.ds(at, rows, stride=2), :] * s
        for j in range(2):
            ext[6 + j : 7 + j, lanes] = back[pl.ds(at + 2 * (rows - 2 + j) + 1, 1), :] * s
            ext[8 + rows + j : 9 + rows + j, lanes] = back[pl.ds(at + 2 * j + 1, 1), :] * s

    total = rows + 16
    m = jnp.concatenate(
        [jnp.broadcast_to(aux[4:5, :], (8, width)), mask[...], jnp.broadcast_to(aux[5:6, :], (8, width))], 0
    )

    def lateral(x):
        return pltpu.roll(x, 1, 0) + pltpu.roll(x, total - 1, 0) + beside(x)

    d = ext[...]
    one0 = m * ((1.0 - 4.0 * h0 - v) * d + h0 * lateral(d))
    one1 = m * (v * d)
    two0 = (1.0 - 4.0 * h0 - v) * one0 + h0 * lateral(one0) + v * one1
    two1 = (1.0 - 4.0 * h1 - 2.0 * v) * one1 + h1 * lateral(one1) + v * one0
    two2 = v * one1
    for level, two in enumerate((two0, two1, two2)):
        three[level] = base[level] + (m * two)[8 : 8 + rows]
    copy = pltpu.make_async_copy(three, out.at[0, pl.ds(0, 3)], sem)
    copy.start()
    copy.wait()


def add_flux(base, back, mask, aux, whole):
    vmem = pl.BlockSpec(memory_space=pltpu.VMEM)
    hbm = pl.BlockSpec(memory_space=pltpu.HBM)
    rows, width = mask.shape
    return pl.pallas_call(
        add_kernel,
        out_shape=jax.ShapeDtypeStruct(whole.shape, jnp.float32),
        in_specs=[vmem, vmem, vmem, vmem, hbm],
        out_specs=hbm,
        scratch_shapes=[pltpu.VMEM((rows + 16, width), jnp.float32), pltpu.VMEM(base.shape, jnp.float32), pltpu.SemaphoreType.DMA],
        input_output_aliases={4: 0},
        compiler_params=pltpu.CompilerParams(vmem_limit_bytes=2 * MIB),
        cost_estimate=pl.CostEstimate(flops=30 * mask.size, bytes_accessed=32 * mask.size, transcendentals=0),
        name="add",
    )(base, back, mask, aux, whole)


def per_device(state, horiz_rate, vert_rate, sea_mask, exchange_coef, partner):
    ntile = lax.axis_size("tile")
    fields, hz, vt = state[0], horiz_rate[0], vert_rate[0]
    outgoing, scale = prep(fields, exchange_coef, sea_mask)
    got = lax.all_to_all(outgoing, BOTH, 0, 0, tiled=True)
    pieces = flux_pieces(partner, got)
    back = lax.all_to_all(pieces, BOTH, 0, 0, tiled=True)

    sent_near, sent_far = edges(fields, sea_mask)
    got_near = lax.ppermute(sent_near, "tile", [(i, i ^ 1) for i in range(ntile)])
    got_far = lax.ppermute(sent_far, "tile", [(i, (i + 2 * (i % 2) - 1) % ntile) for i in range(ntile)])
    whole, base, aux = mix(fields, hz, vt, sent_near, sent_far, got_near, got_far, scale)
    return add_flux(base, back, scale, aux, whole)[None]


def solution(mesh):
    placed = (
        P("comp", None, None, "tile", None),
        P("comp", None, None),
        P("comp", None),
        P("tile", None),
        P("tile", None),
        P(),
    )
    return jax.shard_map(
        per_device,
        mesh=mesh,
        in_specs=placed,
        out_specs=P("comp", None, None, "tile", None),
        check_vma=False,
    )
```

```python
import functools

import jax
import jax.numpy as jnp
from jax import lax
from jax.experimental import pallas as pl
from jax.experimental.pallas import tpu as pltpu
from jax.sharding import PartitionSpec as P

BOTH = ("comp", "tile")
BLOCK = 16
MIB = 1 << 20


def row_ids(rows, width):
    return lax.broadcasted_iota(jnp.int32, (rows, width), 0)


def beside(x):
    half = x.shape[-1] // 2
    a, b = x[:, :half], x[:, half:]
    lane = lax.broadcasted_iota(jnp.int32, a.shape, 1)
    first, last = lane == 0, lane == half - 1
    ra, rb = pltpu.roll(a, 1, 1), pltpu.roll(b, 1, 1)
    la, lb = pltpu.roll(a, half - 1, 1), pltpu.roll(b, half - 1, 1)
    left = jnp.where(first, rb, ra) + jnp.where(last, lb, la)
    right = jnp.where(first, ra, rb) + jnp.where(last, la, lb)
    return jnp.concatenate([left, right], 1)


def mix_kernel(
    hz_any, vt_any, state, sent_near, sent_far, got_near, got_far, mask, out, base, aux,
    mine, halo, strip_sem, hz, vt, hcol, raw, s0, s1, res, edge, split, wet, rate_sem, in_sem, out_sem,
):
    planes, rows, width = state.shape
    fields, levels = hz.shape
    blocks = planes // BLOCK
    half = width // 2
    sides = [pl.ds(k * half, half) for k in range(2)]

    def load(at, q):
        return [
            pltpu.make_async_copy(state.at[at, :, lanes], raw.at[k, at], in_sem.at[q, k])
            for k, lanes in enumerate(sides)
        ]

    def store(at):
        return [
            pltpu.make_async_copy(res.at[k, at], out.at[at, :, lanes], out_sem.at[k])
            for k, lanes in enumerate(sides)
        ]

    def ready(q):
        if isinstance(q, int):
            lo, hi = q * BLOCK + (q > 0), min((q + 1) * BLOCK + 1, planes)
            return load(pl.ds(lo, hi - lo), q)
        return load(pl.ds(q * BLOCK + 1, BLOCK), q)

    def leave(lo, count):
        for copy in store(pl.ds(lo, count)):
            copy.start()

    odd = lax.axis_index("tile") % 2
    strips = [
        pltpu.make_async_copy(src, dst.at[slot], strip_sem.at[i])
        for i, (src, dst, slot) in enumerate(
            ((sent_near, mine, 1 - odd), (sent_far, mine, odd), (got_near, halo, 1 - odd), (got_far, halo, odd))
        )
    ]
    for copy in strips:
        copy.start()
    rates = [pltpu.make_async_copy(hz_any, hz, rate_sem.at[0]), pltpu.make_async_copy(vt_any, vt, rate_sem.at[1])]
    for copy in rates:
        copy.start()

    for q in range(blocks):
        for copy in ready(q):
            copy.start()

    for copy in rates:
        copy.wait()

    for p in range(planes):
        hcol[p : p + 1, :] = jnp.full((1, half), hz[p // levels, p % levels], jnp.float32)

    for copy in strips:
        copy.wait()
    mine_first, mine_last, before, after = mine.at[0], mine.at[1], halo.at[0], halo.at[1]
    for j in range(4):
        aux[j : j + 1, :] = jnp.full((1, width), (hz[0, 0], hz[0, 1], vt[0], vt[0])[j], jnp.float32)
    aux[4:5, :] = before[1, planes : planes + 1, :]
    aux[5:6, :] = after[0, planes : planes + 1, :]

    level = row_ids(levels, width)
    for side, (x2, x1, x0, m) in enumerate(
        (
            (before.at[0], before.at[1], mine_first.at[0], before[1, planes : planes + 1, :]),
            (after.at[1], after.at[0], mine_last.at[1], after[0, planes : planes + 1, :]),
        )
    ):
        for f in range(fields):
            at = pl.ds(f * levels, levels)
            x = x1[at, :]
            lap = x2[at, :] + x0[at, :] + beside(x)
            below = jnp.where(level == 0, x, pltpu.roll(x, 1, 0))
            above = jnp.where(level == levels - 1, x, pltpu.roll(x, levels - 1, 0))
            h = jnp.concatenate([hcol[at, :]] * 2, 1)
            v = vt[f]
            new = x * (1.0 - 4.0 * h - 2.0 * v) + h * lap + v * (above + below)
            edge[side, at, :] = new * m

    row = row_ids(8, width)
    top, bottom = row == 0, row == 7
    nrow = rows // 8

    for k, lanes in enumerate(sides):
        split[k] = mask[:, lanes]
        for r in range(nrow):
            wet[pl.ds(8 * r, 8), lanes] = split[k, pl.ds(r, 8, stride=nrow), :]

    def pack(p):
        for r in range(nrow):
            s0[p, pl.ds(8 * r, 8), :] = jnp.concatenate([raw[k, p, pl.ds(r, 8, stride=nrow), :] for k in range(2)], 1)

    def substep(src, p, lo, hi, ahead, behind):
        f = p // levels
        h, v = hz[f, p % levels], vt[f]
        c0 = 1.0 - 4.0 * h - 2.0 * v
        x = [src[p, pl.ds(8 * r, 8), :] for r in range(nrow)]
        above = jnp.where(top, jnp.broadcast_to(ahead[pl.ds(p, 1), :], (8, width)), pltpu.roll(x[-1], 1, 0))
        under = jnp.where(bottom, jnp.broadcast_to(behind[pl.ds(p, 1), :], (8, width)), pltpu.roll(x[0], 7, 0))
        for r in range(nrow):
            at = pl.ds(8 * r, 8)
            near = (x[r - 1] if r else above) + (x[r + 1] if r < nrow - 1 else under)
            vert = src[lo, at, :] + src[hi, at, :]
            new = x[r] * c0 + h * (near + beside(x[r])) + v * vert
            yield r, new * wet[at, :]

    def first(start, i):
        p = start + i
        pack(p + 1 if i < BLOCK - 1 else jnp.minimum(p + 1, planes - 1))
        lo = p - 1 if i else jnp.where(p % levels == 0, p, p - 1)
        hi = p + 1 if i < BLOCK - 1 else jnp.where(p % levels == levels - 1, p, p + 1)
        for r, new in substep(s0, p, lo, hi, before.at[1], after.at[0]):
            s1[p, pl.ds(8 * r, 8), :] = new

    def second_at(p, lo, hi):
        for r, new in substep(s1, p, lo, hi, edge.at[0], edge.at[1]):
            for k in range(2):
                res[k, p, pl.ds(r, 8, stride=nrow), :] = new[:, k * half : (k + 1) * half]

    def second(start, i):
        p = start + i - 1 if i else jnp.maximum(start - 1, 0)
        lo = p - 1 if i > 1 else jnp.where(p % levels == 0, p, p - 1)
        hi = p + 1 if i else jnp.where(p % levels == levels - 1, p, p + 1)
        second_at(p, lo, hi)

    for copy in ready(0):
        copy.wait()
    pack(0)
    for i in range(BLOCK):
        first(0, i)

    @pl.loop(1, blocks)
    def _(q):
        @pl.when(q < blocks - 1)
        def _():
            for copy in ready(q):
                copy.wait()

        @pl.when(q == blocks - 1)
        def _():
            for copy in ready(blocks - 1):
                copy.wait()

        now = q * BLOCK
        for i in range(BLOCK):
            second(now - BLOCK, i)
        for i in range(BLOCK):
            first(now, i)

        @pl.when(q > 1)
        def _():
            leave(now - BLOCK - 1, BLOCK)

        @pl.when(q == 1)
        def _():
            leave(0, BLOCK - 1)
            for k, lanes in enumerate(sides):
                base[:, :, lanes] = res[k, 0:3]

    done = planes - BLOCK - 1
    for i in range(BLOCK):
        second(planes - BLOCK, i)
        if i == BLOCK // 2:
            leave(done, i + 1)
            done += i + 1
    second_at(planes - 1, planes - 2, planes - 1)
    leave(done, planes - done)
    for copy in store(pl.ds(0, planes)):
        copy.wait()


def mix(fields, hz, vt, sent_near, sent_far, got_near, got_far, mask):
    nf, levels, rows, width = fields.shape
    planes = nf * levels
    flat = (planes, rows, width)
    vmem = pl.BlockSpec(memory_space=pltpu.VMEM)
    hbm = pl.BlockSpec(memory_space=pltpu.HBM)
    blocks = planes // BLOCK
    halved = (2, planes, rows, width // 2)
    whole, base, aux = pl.pallas_call(
        mix_kernel,
        out_shape=(
            jax.ShapeDtypeStruct(flat, jnp.float32),
            jax.ShapeDtypeStruct((3, rows, width), jnp.float32),
            jax.ShapeDtypeStruct((8, width), jnp.float32),
        ),
        in_specs=[hbm, hbm, hbm, vmem, vmem, vmem, vmem, vmem],
        out_specs=(hbm, vmem, vmem),
        scratch_shapes=[
            pltpu.VMEM((2, 2, planes + 8, width), jnp.float32),
            pltpu.VMEM((2, 2, planes + 8, width), jnp.float32),
            pltpu.SemaphoreType.DMA((4,)),
            pltpu.SMEM((nf, levels), jnp.float32),
            pltpu.SMEM((nf,), jnp.float32),
            pltpu.VMEM((planes, width // 2), jnp.float32),
            pltpu.VMEM(halved, jnp.float32),
            pltpu.VMEM(flat, jnp.float32),
            pltpu.VMEM(flat, jnp.float32),
            pltpu.VMEM(halved, jnp.float32),
            pltpu.VMEM((2, planes, width), jnp.float32),
            pltpu.VMEM((2, rows, width // 2), jnp.float32),
            pltpu.VMEM((rows, width), jnp.float32),
            pltpu.SemaphoreType.DMA((2,)),
            pltpu.SemaphoreType.DMA((blocks, 2)),
            pltpu.SemaphoreType.DMA((2,)),
        ],
        compiler_params=pltpu.CompilerParams(vmem_limit_bytes=46 * MIB),
        cost_estimate=pl.CostEstimate(flops=26 * fields.size, bytes_accessed=8 * fields.size, transcendentals=0),
        name="mix",
    )(hz, vt, fields.reshape(flat), sent_near, sent_far, got_near, got_far, mask)
    return whole.reshape(fields.shape), base, aux


def prep_kernel(state, coef_hbm, sea_hbm, out, wet, surface, coef, sea, sem):
    rows, width = coef.shape
    half = width // 2
    copies = [
        pltpu.make_async_copy(state.at[0, 0], surface, sem.at[0]),
        pltpu.make_async_copy(coef_hbm, coef, sem.at[1]),
        pltpu.make_async_copy(sea_hbm, sea, sem.at[2]),
    ]
    for copy in copies:
        copy.start()
    for copy in copies:
        copy.wait()
    ocean = sea[...].astype(jnp.float32)
    mine = lax.axis_index("comp") == 0
    second = jnp.where(mine, coef[...], ocean)
    wet[...] = jnp.where(mine, jnp.ones_like(ocean), ocean)
    for k in range(2):
        lanes = slice(k * half, (k + 1) * half)
        out[pl.ds(2 * k * rows, rows, stride=2), :] = surface[:, lanes]
        out[pl.ds(2 * k * rows + 1, rows, stride=2), :] = second[:, lanes]


def prep(fields, coef, sea):
    vmem = pl.BlockSpec(memory_space=pltpu.VMEM)
    hbm = pl.BlockSpec(memory_space=pltpu.HBM)
    rows, width = coef.shape
    return pl.pallas_call(
        prep_kernel,
        out_shape=(
            jax.ShapeDtypeStruct((4 * rows, width // 2), jnp.float32),
            jax.ShapeDtypeStruct((rows, width), jnp.float32),
        ),
        in_specs=[hbm, hbm, hbm],
        out_specs=(vmem, vmem),
        scratch_shapes=[
            pltpu.VMEM((rows, width), jnp.float32),
            pltpu.VMEM((rows, width), jnp.float32),
            pltpu.VMEM((rows, width), jnp.int32),
            pltpu.SemaphoreType.DMA((3,)),
        ],
        compiler_params=pltpu.CompilerParams(vmem_limit_bytes=60 * MIB),
        cost_estimate=pl.CostEstimate(flops=3 * coef.size, bytes_accessed=24 * coef.size, transcendentals=0),
        name="prep",
    )(fields, coef, sea)


def edge_kernel(state, sea_any, partner_any, near, far, chosen, stage, sea, partner, sem):
    nf, levels, rows, width = state.shape
    planes = nf * levels
    copies = [
        pltpu.make_async_copy(state.at[f, :, pl.ds(at, 8), :], stage.at[side, f], sem.at[side, f])
        for side, at in enumerate((0, rows - 8))
        for f in range(nf)
    ]
    small = [
        pltpu.make_async_copy(sea_any, sea, sem.at[2, 0]),
        pltpu.make_async_copy(partner_any, partner, sem.at[2, 1]),
    ]
    for copy in small + copies:
        copy.start()
    for copy in small:
        copy.wait()
    tiles = chosen.shape[0]
    column = lax.broadcasted_iota(jnp.int32, (1, tiles), 1)
    for t in range(tiles):
        chosen[t : t + 1, :] = (column == partner[t]).astype(jnp.float32)

    def fill(first, last):
        for side, (out, at) in enumerate(((first, 0), (last, 6))):
            for f in range(nf):
                copies[side * nf + f].wait()
                for j in range(2):
                    for g in range(0, levels, 8):
                        p = f * levels + g
                        out[j, p : p + 8, :] = stage[side, f, g : g + 8, at + j, :]
            for j in range(2):
                row = side * (rows - 2) + j
                wet = jnp.where(lax.axis_index("comp") == 0, 1.0, sea[row : row + 1, :].astype(jnp.float32))
                out[j, planes : planes + 8, :] = jnp.broadcast_to(wet, (8, width))

    even = lax.axis_index("tile") % 2 == 0

    @pl.when(even)
    def _():
        fill(far, near)

    @pl.when(jnp.logical_not(even))
    def _():
        fill(near, far)


def edges(fields, sea, partner):
    vmem = pl.BlockSpec(memory_space=pltpu.VMEM)
    anyw = pl.BlockSpec(memory_space=pl.ANY)
    hbm = pl.BlockSpec(memory_space=pltpu.HBM)
    nf, levels, _, width = fields.shape
    shape = jax.ShapeDtypeStruct((2, nf * levels + 8, width), jnp.float32)
    return pl.pallas_call(
        edge_kernel,
        out_shape=(shape, shape, jax.ShapeDtypeStruct((partner.size, partner.size), jnp.float32)),
        in_specs=[hbm, anyw, anyw],
        out_specs=(vmem, vmem, vmem),
        scratch_shapes=[
            pltpu.VMEM((2, nf, levels, 8, width), jnp.float32),
            pltpu.VMEM(sea.shape, jnp.int32),
            pltpu.SMEM(partner.shape, jnp.int32),
            pltpu.SemaphoreType.DMA((3, nf)),
        ],
        compiler_params=pltpu.CompilerParams(vmem_limit_bytes=46 * MIB),
        cost_estimate=pl.CostEstimate(flops=0, bytes_accessed=4 * MIB, transcendentals=0),
        name="edges",
    )(fields, sea, partner)


def flux_kernel(chosen, got, back):
    tiles, half = chosen.shape[0], got.shape[1]
    odd, even = pl.ds(1, tiles, stride=2), pl.ds(0, tiles, stride=2)
    ocean = jnp.concatenate([got[pl.ds(2 * tiles + k, tiles, stride=2), :] for k in range(2)], 1)
    theirs = jnp.dot(chosen[...], ocean, precision=lax.Precision.HIGHEST, preferred_element_type=jnp.float32)
    flux = got[odd, :] * (got[even, :] - theirs[:, 0:half]) * theirs[:, half:]
    turned = lax.dot_general(
        chosen[...], flux, (((0,), (0,)), ((), ())), precision=lax.Precision.HIGHEST, preferred_element_type=jnp.float32
    )
    shift = jnp.where(lax.axis_index("tile") < 2, tiles - 1, 1)
    back[even, :] = flux
    back[odd, :] = pltpu.roll(flux, shift, 0)
    back[pl.ds(2 * tiles, tiles, stride=2), :] = turned
    back[pl.ds(2 * tiles + 1, tiles, stride=2), :] = pltpu.roll(turned, shift, 0)


def flux_pieces(chosen, got):
    vmem = pl.BlockSpec(memory_space=pltpu.VMEM)
    return pl.pallas_call(
        flux_kernel,
        out_shape=jax.ShapeDtypeStruct(got.shape, jnp.float32),
        in_specs=[vmem, vmem],
        out_specs=vmem,
        compiler_params=pltpu.CompilerParams(vmem_limit_bytes=2 * MIB),
        cost_estimate=pl.CostEstimate(flops=3 * 10**10, bytes_accessed=8 * got.size, transcendentals=0),
        name="flux",
    )(chosen, got)


def add_kernel(base, back, mask, aux, whole, out, ext, three, sem):
    del whole
    rows, width = mask.shape
    half = width // 2
    s = jnp.where(lax.axis_index("comp") == 0, -1.0, 1.0).astype(jnp.float32)
    h0, h1, v = (aux[j : j + 1, :] for j in range(3))
    zero_pad = jnp.zeros((8, width), jnp.float32)
    ext[0:8, :] = zero_pad
    ext[8 + rows : 16 + rows, :] = zero_pad
    for k in range(2):
        lanes = pl.ds(k * half, half)
        at = 2 * k * rows
        ext[8 : 8 + rows, lanes] = back[pl.ds(at, rows, stride=2), :] * s
        for j in range(2):
            ext[6 + j : 7 + j, lanes] = back[pl.ds(at + 2 * (rows - 2 + j) + 1, 1), :] * s
            ext[8 + rows + j : 9 + rows + j, lanes] = back[pl.ds(at + 2 * j + 1, 1), :] * s

    total = rows + 16
    m = jnp.concatenate(
        [jnp.broadcast_to(aux[4:5, :], (8, width)), mask[...], jnp.broadcast_to(aux[5:6, :], (8, width))], 0
    )

    def lateral(x):
        return pltpu.roll(x, 1, 0) + pltpu.roll(x, total - 1, 0) + beside(x)

    d = ext[...]
    one0 = m * ((1.0 - 4.0 * h0 - v) * d + h0 * lateral(d))
    one1 = m * (v * d)
    two0 = (1.0 - 4.0 * h0 - v) * one0 + h0 * lateral(one0) + v * one1
    two1 = (1.0 - 4.0 * h1 - 2.0 * v) * one1 + h1 * lateral(one1) + v * one0
    two2 = v * one1
    for level, two in enumerate((two0, two1, two2)):
        three[level] = base[level] + (m * two)[8 : 8 + rows]
    copy = pltpu.make_async_copy(three, out.at[0, pl.ds(0, 3)], sem)
    copy.start()
    copy.wait()


def add_flux(base, back, mask, aux, whole):
    vmem = pl.BlockSpec(memory_space=pltpu.VMEM)
    hbm = pl.BlockSpec(memory_space=pltpu.HBM)
    rows, width = mask.shape
    return pl.pallas_call(
        add_kernel,
        out_shape=jax.ShapeDtypeStruct(whole.shape, jnp.float32),
        in_specs=[vmem, vmem, vmem, vmem, hbm],
        out_specs=hbm,
        scratch_shapes=[pltpu.VMEM((rows + 16, width), jnp.float32), pltpu.VMEM(base.shape, jnp.float32), pltpu.SemaphoreType.DMA],
        input_output_aliases={4: 0},
        compiler_params=pltpu.CompilerParams(vmem_limit_bytes=2 * MIB),
        cost_estimate=pl.CostEstimate(flops=30 * mask.size, bytes_accessed=32 * mask.size, transcendentals=0),
        name="add",
    )(base, back, mask, aux, whole)


def per_device(state, horiz_rate, vert_rate, sea_mask, exchange_coef, partner):
    ntile = lax.axis_size("tile")
    fields, hz, vt = state[0], horiz_rate[0], vert_rate[0]
    outgoing, scale = prep(fields, exchange_coef, sea_mask)
    got = lax.all_to_all(outgoing, BOTH, 0, 0, tiled=True)
    sent_near, sent_far, chosen = edges(fields, sea_mask, partner)
    pieces = flux_pieces(chosen, got)
    back = lax.all_to_all(pieces, BOTH, 0, 0, tiled=True)

    got_near = lax.ppermute(sent_near, "tile", [(i, i ^ 1) for i in range(ntile)])
    got_far = lax.ppermute(sent_far, "tile", [(i, (i + 2 * (i % 2) - 1) % ntile) for i in range(ntile)])
    whole, base, aux = mix(fields, hz, vt, sent_near, sent_far, got_near, got_far, scale)
    return add_flux(base, back, scale, aux, whole)[None]


def solution(mesh):
    placed = (
        P("comp", None, None, "tile", None),
        P("comp", None, None),
        P("comp", None),
        P("tile", None),
        P("tile", None),
        P(),
    )
    return jax.shard_map(
        per_device,
        mesh=mesh,
        in_specs=placed,
        out_specs=P("comp", None, None, "tile", None),
        check_vma=False,
    )
```

```python
import functools

import jax
import jax.numpy as jnp
from jax import lax
from jax.experimental import pallas as pl
from jax.experimental.pallas import tpu as pltpu
from jax.sharding import PartitionSpec as P

BOTH = ("comp", "tile")
BLOCK = 32
PART = 16
MIB = 1 << 20


def row_ids(rows, width):
    return lax.broadcasted_iota(jnp.int32, (rows, width), 0)


def beside(x):
    half = x.shape[-1] // 2
    a, b = x[:, :half], x[:, half:]
    lane = lax.broadcasted_iota(jnp.int32, a.shape, 1)
    first, last = lane == 0, lane == half - 1
    ra, rb = pltpu.roll(a, 1, 1), pltpu.roll(b, 1, 1)
    la, lb = pltpu.roll(a, half - 1, 1), pltpu.roll(b, half - 1, 1)
    left = jnp.where(first, rb, ra) + jnp.where(last, lb, la)
    right = jnp.where(first, ra, rb) + jnp.where(last, la, lb)
    return jnp.concatenate([left, right], 1)


def mix_kernel(
    hz_any, vt_any, state, sent_near, sent_far, got_near, got_far, mask, out, base, aux,
    mine, halo, strip_sem, hz, vt, hcol, raw, s0, s1, res, edge, split, wet, rate_sem, in_sem, out_sem,
):
    planes, rows, width = state.shape
    fields, levels = hz.shape
    blocks = planes // BLOCK
    half = width // 2
    sides = [pl.ds(k * half, half) for k in range(2)]

    def load(at, q):
        return [
            pltpu.make_async_copy(state.at[at, :, lanes], raw.at[k, at], in_sem.at[q, k])
            for k, lanes in enumerate(sides)
        ]

    def store(at):
        return [
            pltpu.make_async_copy(res.at[k, at], out.at[at, :, lanes], out_sem.at[k])
            for k, lanes in enumerate(sides)
        ]

    def ready(q):
        if isinstance(q, int):
            lo, hi = q * PART + (q > 0), min((q + 1) * PART + 1, planes)
            return load(pl.ds(lo, hi - lo), q)
        return load(pl.ds(q * PART + 1, PART), q)

    def leave(lo, count):
        for copy in store(pl.ds(lo, count)):
            copy.start()

    odd = lax.axis_index("tile") % 2
    strips = [
        pltpu.make_async_copy(src, dst.at[slot], strip_sem.at[i])
        for i, (src, dst, slot) in enumerate(
            ((sent_near, mine, 1 - odd), (sent_far, mine, odd), (got_near, halo, 1 - odd), (got_far, halo, odd))
        )
    ]
    for copy in strips:
        copy.start()
    rates = [pltpu.make_async_copy(hz_any, hz, rate_sem.at[0]), pltpu.make_async_copy(vt_any, vt, rate_sem.at[1])]
    for copy in rates:
        copy.start()

    parts = planes // PART
    for q in range(parts):
        for copy in ready(q):
            copy.start()

    for copy in rates:
        copy.wait()

    for p in range(planes):
        hcol[p : p + 1, :] = jnp.full((1, half), hz[p // levels, p % levels], jnp.float32)

    for copy in strips:
        copy.wait()
    mine_first, mine_last, before, after = mine.at[0], mine.at[1], halo.at[0], halo.at[1]
    for j in range(4):
        aux[j : j + 1, :] = jnp.full((1, width), (hz[0, 0], hz[0, 1], vt[0], vt[0])[j], jnp.float32)
    aux[4:5, :] = before[1, planes : planes + 1, :]
    aux[5:6, :] = after[0, planes : planes + 1, :]

    level = row_ids(levels, width)
    for side, (x2, x1, x0, m) in enumerate(
        (
            (before.at[0], before.at[1], mine_first.at[0], before[1, planes : planes + 1, :]),
            (after.at[1], after.at[0], mine_last.at[1], after[0, planes : planes + 1, :]),
        )
    ):
        for f in range(fields):
            at = pl.ds(f * levels, levels)
            x = x1[at, :]
            lap = x2[at, :] + x0[at, :] + beside(x)
            below = jnp.where(level == 0, x, pltpu.roll(x, 1, 0))
            above = jnp.where(level == levels - 1, x, pltpu.roll(x, levels - 1, 0))
            h = jnp.concatenate([hcol[at, :]] * 2, 1)
            v = vt[f]
            new = x * (1.0 - 4.0 * h - 2.0 * v) + h * lap + v * (above + below)
            edge[side, at, :] = new * m

    row = row_ids(8, width)
    top, bottom = row == 0, row == 7
    nrow = rows // 8

    for k, lanes in enumerate(sides):
        split[k] = mask[:, lanes]
        for r in range(nrow):
            wet[pl.ds(8 * r, 8), lanes] = split[k, pl.ds(r, 8, stride=nrow), :]

    def pack(p):
        for r in range(nrow):
            s0[p, pl.ds(8 * r, 8), :] = jnp.concatenate([raw[k, p, pl.ds(r, 8, stride=nrow), :] for k in range(2)], 1)

    def substep(src, p, lo, hi, ahead, behind):
        f = p // levels
        h, v = hz[f, p % levels], vt[f]
        c0 = 1.0 - 4.0 * h - 2.0 * v
        x = [src[p, pl.ds(8 * r, 8), :] for r in range(nrow)]
        above = jnp.where(top, jnp.broadcast_to(ahead[pl.ds(p, 1), :], (8, width)), pltpu.roll(x[-1], 1, 0))
        under = jnp.where(bottom, jnp.broadcast_to(behind[pl.ds(p, 1), :], (8, width)), pltpu.roll(x[0], 7, 0))
        for r in range(nrow):
            at = pl.ds(8 * r, 8)
            near = (x[r - 1] if r else above) + (x[r + 1] if r < nrow - 1 else under)
            vert = src[lo, at, :] + src[hi, at, :]
            new = x[r] * c0 + h * (near + beside(x[r])) + v * vert
            yield r, new * wet[at, :]

    def first(start, i):
        p = start + i
        pack(p + 1 if i < BLOCK - 1 else jnp.minimum(p + 1, planes - 1))
        lo = p - 1 if i else jnp.where(p % levels == 0, p, p - 1)
        hi = p + 1 if i < BLOCK - 1 else jnp.where(p % levels == levels - 1, p, p + 1)
        for r, new in substep(s0, p, lo, hi, before.at[1], after.at[0]):
            s1[p, pl.ds(8 * r, 8), :] = new

    def second_at(p, lo, hi):
        for r, new in substep(s1, p, lo, hi, edge.at[0], edge.at[1]):
            for k in range(2):
                res[k, p, pl.ds(r, 8, stride=nrow), :] = new[:, k * half : (k + 1) * half]

    def second(start, i):
        p = start + i - 1 if i else jnp.maximum(start - 1, 0)
        lo = p - 1 if i > 1 else jnp.where(p % levels == 0, p, p - 1)
        hi = p + 1 if i else jnp.where(p % levels == levels - 1, p, p + 1)
        second_at(p, lo, hi)

    for copy in ready(0):
        copy.wait()
    pack(0)
    for i in range(BLOCK):
        if i and i % PART == 0:
            for copy in ready(i // PART):
                copy.wait()
        first(0, i)

    @pl.loop(1, blocks)
    def _(q):
        for j in range(BLOCK // PART - 1):
            for copy in ready(q * (BLOCK // PART) + j):
                copy.wait()

        @pl.when(q < blocks - 1)
        def _():
            for copy in ready((q + 1) * (BLOCK // PART) - 1):
                copy.wait()

        @pl.when(q == blocks - 1)
        def _():
            for copy in ready(parts - 1):
                copy.wait()

        now = q * BLOCK
        for i in range(BLOCK):
            second(now - BLOCK, i)
        for i in range(BLOCK):
            first(now, i)

        @pl.when(q > 1)
        def _():
            leave(now - BLOCK - 1, BLOCK)

        @pl.when(q == 1)
        def _():
            leave(0, BLOCK - 1)
            for k, lanes in enumerate(sides):
                base[:, :, lanes] = res[k, 0:3]

    done = planes - BLOCK - 1
    for i in range(BLOCK):
        second(planes - BLOCK, i)
        if i in (BLOCK // 2, 3 * BLOCK // 4):
            leave(done, planes - BLOCK + i - done)
            done = planes - BLOCK + i
    second_at(planes - 1, planes - 2, planes - 1)
    leave(done, planes - done)
    for copy in store(pl.ds(0, planes)):
        copy.wait()


def mix(fields, hz, vt, sent_near, sent_far, got_near, got_far, mask):
    nf, levels, rows, width = fields.shape
    planes = nf * levels
    flat = (planes, rows, width)
    vmem = pl.BlockSpec(memory_space=pltpu.VMEM)
    hbm = pl.BlockSpec(memory_space=pltpu.HBM)
    halved = (2, planes, rows, width // 2)
    whole, base, aux = pl.pallas_call(
        mix_kernel,
        out_shape=(
            jax.ShapeDtypeStruct(flat, jnp.float32),
            jax.ShapeDtypeStruct((3, rows, width), jnp.float32),
            jax.ShapeDtypeStruct((8, width), jnp.float32),
        ),
        in_specs=[hbm, hbm, hbm, vmem, vmem, vmem, vmem, vmem],
        out_specs=(hbm, vmem, vmem),
        scratch_shapes=[
            pltpu.VMEM((2, 2, planes + 8, width), jnp.float32),
            pltpu.VMEM((2, 2, planes + 8, width), jnp.float32),
            pltpu.SemaphoreType.DMA((4,)),
            pltpu.SMEM((nf, levels), jnp.float32),
            pltpu.SMEM((nf,), jnp.float32),
            pltpu.VMEM((planes, width // 2), jnp.float32),
            pltpu.VMEM(halved, jnp.float32),
            pltpu.VMEM(flat, jnp.float32),
            pltpu.VMEM(flat, jnp.float32),
            pltpu.VMEM(halved, jnp.float32),
            pltpu.VMEM((2, planes, width), jnp.float32),
            pltpu.VMEM((2, rows, width // 2), jnp.float32),
            pltpu.VMEM((rows, width), jnp.float32),
            pltpu.SemaphoreType.DMA((2,)),
            pltpu.SemaphoreType.DMA((planes // PART, 2)),
            pltpu.SemaphoreType.DMA((2,)),
        ],
        compiler_params=pltpu.CompilerParams(vmem_limit_bytes=46 * MIB),
        cost_estimate=pl.CostEstimate(flops=26 * fields.size, bytes_accessed=8 * fields.size, transcendentals=0),
        name="mix",
    )(hz, vt, fields.reshape(flat), sent_near, sent_far, got_near, got_far, mask)
    return whole.reshape(fields.shape), base, aux


def prep_kernel(state, coef_hbm, sea_hbm, out, wet, surface, coef, sea, sem):
    rows, width = coef.shape
    half = width // 2
    copies = [
        pltpu.make_async_copy(state.at[0, 0], surface, sem.at[0]),
        pltpu.make_async_copy(coef_hbm, coef, sem.at[1]),
        pltpu.make_async_copy(sea_hbm, sea, sem.at[2]),
    ]
    for copy in copies:
        copy.start()
    for copy in copies:
        copy.wait()
    ocean = sea[...].astype(jnp.float32)
    mine = lax.axis_index("comp") == 0
    second = jnp.where(mine, coef[...], ocean)
    wet[...] = jnp.where(mine, jnp.ones_like(ocean), ocean)
    for k in range(2):
        lanes = slice(k * half, (k + 1) * half)
        out[pl.ds(2 * k * rows, rows, stride=2), :] = surface[:, lanes]
        out[pl.ds(2 * k * rows + 1, rows, stride=2), :] = second[:, lanes]


def prep(fields, coef, sea):
    vmem = pl.BlockSpec(memory_space=pltpu.VMEM)
    hbm = pl.BlockSpec(memory_space=pltpu.HBM)
    rows, width = coef.shape
    return pl.pallas_call(
        prep_kernel,
        out_shape=(
            jax.ShapeDtypeStruct((4 * rows, width // 2), jnp.float32),
            jax.ShapeDtypeStruct((rows, width), jnp.float32),
        ),
        in_specs=[hbm, hbm, hbm],
        out_specs=(vmem, vmem),
        scratch_shapes=[
            pltpu.VMEM((rows, width), jnp.float32),
            pltpu.VMEM((rows, width), jnp.float32),
            pltpu.VMEM((rows, width), jnp.int32),
            pltpu.SemaphoreType.DMA((3,)),
        ],
        compiler_params=pltpu.CompilerParams(vmem_limit_bytes=60 * MIB),
        cost_estimate=pl.CostEstimate(flops=3 * coef.size, bytes_accessed=24 * coef.size, transcendentals=0),
        name="prep",
    )(fields, coef, sea)


def edge_kernel(state, sea_any, partner_any, near, far, chosen, stage, sea, partner, sem):
    nf, levels, rows, width = state.shape
    planes = nf * levels
    copies = [
        pltpu.make_async_copy(state.at[f, :, pl.ds(at, 8), :], stage.at[side, f], sem.at[side, f])
        for side, at in enumerate((0, rows - 8))
        for f in range(nf)
    ]
    small = [
        pltpu.make_async_copy(sea_any, sea, sem.at[2, 0]),
        pltpu.make_async_copy(partner_any, partner, sem.at[2, 1]),
    ]
    for copy in small + copies:
        copy.start()
    for copy in small:
        copy.wait()
    tiles = chosen.shape[0]
    column = lax.broadcasted_iota(jnp.int32, (1, tiles), 1)
    for t in range(tiles):
        chosen[t : t + 1, :] = (column == partner[t]).astype(jnp.float32)

    def fill(first, last):
        for side, (out, at) in enumerate(((first, 0), (last, 6))):
            for f in range(nf):
                copies[side * nf + f].wait()
                for j in range(2):
                    for g in range(0, levels, 8):
                        p = f * levels + g
                        out[j, p : p + 8, :] = stage[side, f, g : g + 8, at + j, :]
            for j in range(2):
                row = side * (rows - 2) + j
                wet = jnp.where(lax.axis_index("comp") == 0, 1.0, sea[row : row + 1, :].astype(jnp.float32))
                out[j, planes : planes + 8, :] = jnp.broadcast_to(wet, (8, width))

    even = lax.axis_index("tile") % 2 == 0

    @pl.when(even)
    def _():
        fill(far, near)

    @pl.when(jnp.logical_not(even))
    def _():
        fill(near, far)


def edges(fields, sea, partner):
    vmem = pl.BlockSpec(memory_space=pltpu.VMEM)
    anyw = pl.BlockSpec(memory_space=pl.ANY)
    hbm = pl.BlockSpec(memory_space=pltpu.HBM)
    nf, levels, _, width = fields.shape
    shape = jax.ShapeDtypeStruct((2, nf * levels + 8, width), jnp.float32)
    return pl.pallas_call(
        edge_kernel,
        out_shape=(shape, shape, jax.ShapeDtypeStruct((partner.size, partner.size), jnp.float32)),
        in_specs=[hbm, anyw, anyw],
        out_specs=(vmem, vmem, vmem),
        scratch_shapes=[
            pltpu.VMEM((2, nf, levels, 8, width), jnp.float32),
            pltpu.VMEM(sea.shape, jnp.int32),
            pltpu.SMEM(partner.shape, jnp.int32),
            pltpu.SemaphoreType.DMA((3, nf)),
        ],
        compiler_params=pltpu.CompilerParams(vmem_limit_bytes=46 * MIB),
        cost_estimate=pl.CostEstimate(flops=0, bytes_accessed=4 * MIB, transcendentals=0),
        name="edges",
    )(fields, sea, partner)


def flux_kernel(chosen, got, back):
    tiles, half = chosen.shape[0], got.shape[1]
    odd, even = pl.ds(1, tiles, stride=2), pl.ds(0, tiles, stride=2)
    ocean = jnp.concatenate([got[pl.ds(2 * tiles + k, tiles, stride=2), :] for k in range(2)], 1)
    theirs = jnp.dot(chosen[...], ocean, precision=lax.Precision.HIGHEST, preferred_element_type=jnp.float32)
    flux = got[odd, :] * (got[even, :] - theirs[:, 0:half]) * theirs[:, half:]
    turned = lax.dot_general(
        chosen[...], flux, (((0,), (0,)), ((), ())), precision=lax.Precision.HIGHEST, preferred_element_type=jnp.float32
    )
    shift = jnp.where(lax.axis_index("tile") < 2, tiles - 1, 1)
    back[even, :] = flux
    back[odd, :] = pltpu.roll(flux, shift, 0)
    back[pl.ds(2 * tiles, tiles, stride=2), :] = turned
    back[pl.ds(2 * tiles + 1, tiles, stride=2), :] = pltpu.roll(turned, shift, 0)


def flux_pieces(chosen, got):
    vmem = pl.BlockSpec(memory_space=pltpu.VMEM)
    return pl.pallas_call(
        flux_kernel,
        out_shape=jax.ShapeDtypeStruct(got.shape, jnp.float32),
        in_specs=[vmem, vmem],
        out_specs=vmem,
        compiler_params=pltpu.CompilerParams(vmem_limit_bytes=2 * MIB),
        cost_estimate=pl.CostEstimate(flops=3 * 10**10, bytes_accessed=8 * got.size, transcendentals=0),
        name="flux",
    )(chosen, got)


def add_kernel(base, back, mask, aux, whole, out, ext, three, sem):
    del whole
    rows, width = mask.shape
    half = width // 2
    s = jnp.where(lax.axis_index("comp") == 0, -1.0, 1.0).astype(jnp.float32)
    h0, h1, v = (aux[j : j + 1, :] for j in range(3))
    zero_pad = jnp.zeros((8, width), jnp.float32)
    ext[0:8, :] = zero_pad
    ext[8 + rows : 16 + rows, :] = zero_pad
    for k in range(2):
        lanes = pl.ds(k * half, half)
        at = 2 * k * rows
        ext[8 : 8 + rows, lanes] = back[pl.ds(at, rows, stride=2), :] * s
        for j in range(2):
            ext[6 + j : 7 + j, lanes] = back[pl.ds(at + 2 * (rows - 2 + j) + 1, 1), :] * s
            ext[8 + rows + j : 9 + rows + j, lanes] = back[pl.ds(at + 2 * j + 1, 1), :] * s

    total = rows + 16
    m = jnp.concatenate(
        [jnp.broadcast_to(aux[4:5, :], (8, width)), mask[...], jnp.broadcast_to(aux[5:6, :], (8, width))], 0
    )

    def lateral(x):
        return pltpu.roll(x, 1, 0) + pltpu.roll(x, total - 1, 0) + beside(x)

    d = ext[...]
    one0 = m * ((1.0 - 4.0 * h0 - v) * d + h0 * lateral(d))
    one1 = m * (v * d)
    two0 = (1.0 - 4.0 * h0 - v) * one0 + h0 * lateral(one0) + v * one1
    two1 = (1.0 - 4.0 * h1 - 2.0 * v) * one1 + h1 * lateral(one1) + v * one0
    two2 = v * one1
    for level, two in enumerate((two0, two1, two2)):
        three[level] = base[level] + (m * two)[8 : 8 + rows]
    copy = pltpu.make_async_copy(three, out.at[0, pl.ds(0, 3)], sem)
    copy.start()
    copy.wait()


def add_flux(base, back, mask, aux, whole):
    vmem = pl.BlockSpec(memory_space=pltpu.VMEM)
    hbm = pl.BlockSpec(memory_space=pltpu.HBM)
    rows, width = mask.shape
    return pl.pallas_call(
        add_kernel,
        out_shape=jax.ShapeDtypeStruct(whole.shape, jnp.float32),
        in_specs=[vmem, vmem, vmem, vmem, hbm],
        out_specs=hbm,
        scratch_shapes=[pltpu.VMEM((rows + 16, width), jnp.float32), pltpu.VMEM(base.shape, jnp.float32), pltpu.SemaphoreType.DMA],
        input_output_aliases={4: 0},
        compiler_params=pltpu.CompilerParams(vmem_limit_bytes=2 * MIB),
        cost_estimate=pl.CostEstimate(flops=30 * mask.size, bytes_accessed=32 * mask.size, transcendentals=0),
        name="add",
    )(base, back, mask, aux, whole)


def per_device(state, horiz_rate, vert_rate, sea_mask, exchange_coef, partner):
    ntile = lax.axis_size("tile")
    fields, hz, vt = state[0], horiz_rate[0], vert_rate[0]
    outgoing, scale = prep(fields, exchange_coef, sea_mask)
    got = lax.all_to_all(outgoing, BOTH, 0, 0, tiled=True)
    sent_near, sent_far, chosen = edges(fields, sea_mask, partner)
    pieces = flux_pieces(chosen, got)
    back = lax.all_to_all(pieces, BOTH, 0, 0, tiled=True)

    got_near = lax.ppermute(sent_near, "tile", [(i, i ^ 1) for i in range(ntile)])
    got_far = lax.ppermute(sent_far, "tile", [(i, (i + 2 * (i % 2) - 1) % ntile) for i in range(ntile)])
    whole, base, aux = mix(fields, hz, vt, sent_near, sent_far, got_near, got_far, scale)
    return add_flux(base, back, scale, aux, whole)[None]


def solution(mesh):
    placed = (
        P("comp", None, None, "tile", None),
        P("comp", None, None),
        P("comp", None),
        P("tile", None),
        P("tile", None),
        P(),
    )
    return jax.shard_map(
        per_device,
        mesh=mesh,
        in_specs=placed,
        out_specs=P("comp", None, None, "tile", None),
        check_vma=False,
    )
```

```python
import functools

import jax
import jax.numpy as jnp
from jax import lax
from jax.experimental import pallas as pl
from jax.experimental.pallas import tpu as pltpu
from jax.sharding import PartitionSpec as P

BOTH = ("comp", "tile")
BLOCK = 32
PART = 16
MIB = 1 << 20


def row_ids(rows, width):
    return lax.broadcasted_iota(jnp.int32, (rows, width), 0)


def beside(x):
    half = x.shape[-1] // 2
    a, b = x[:, :half], x[:, half:]
    lane = lax.broadcasted_iota(jnp.int32, a.shape, 1)
    first, last = lane == 0, lane == half - 1
    ra, rb = pltpu.roll(a, 1, 1), pltpu.roll(b, 1, 1)
    la, lb = pltpu.roll(a, half - 1, 1), pltpu.roll(b, half - 1, 1)
    left = jnp.where(first, rb, ra) + jnp.where(last, lb, la)
    right = jnp.where(first, ra, rb) + jnp.where(last, la, lb)
    return jnp.concatenate([left, right], 1)


def mix_kernel(
    hz_any, vt_any, state, sent_near, sent_far, got_near, got_far, mask, out, base, aux,
    mine, halo, strip_sem, hz, vt, hcol, raw, s0, s1, res, edge, split, wet, rate_sem, in_sem, out_sem,
):
    planes, rows, width = state.shape
    fields, levels = hz.shape
    blocks = planes // BLOCK
    half = width // 2
    sides = [pl.ds(k * half, half) for k in range(2)]

    def load(at, q):
        return [
            pltpu.make_async_copy(state.at[at, :, lanes], raw.at[k, at], in_sem.at[q, k])
            for k, lanes in enumerate(sides)
        ]

    def store(at):
        return [
            pltpu.make_async_copy(res.at[k, at], out.at[at, :, lanes], out_sem.at[k])
            for k, lanes in enumerate(sides)
        ]

    def ready(q):
        if isinstance(q, int):
            lo, hi = q * PART + (q > 0), min((q + 1) * PART + 1, planes)
            return load(pl.ds(lo, hi - lo), q)
        return load(pl.ds(q * PART + 1, PART), q)

    def leave(lo, count):
        for copy in store(pl.ds(lo, count)):
            copy.start()

    odd = lax.axis_index("tile") % 2
    strips = [
        pltpu.make_async_copy(src, dst.at[slot], strip_sem.at[i])
        for i, (src, dst, slot) in enumerate(
            ((sent_near, mine, 1 - odd), (sent_far, mine, odd), (got_near, halo, 1 - odd), (got_far, halo, odd))
        )
    ]
    for copy in strips:
        copy.start()
    rates = [pltpu.make_async_copy(hz_any, hz, rate_sem.at[0]), pltpu.make_async_copy(vt_any, vt, rate_sem.at[1])]
    for copy in rates:
        copy.start()

    parts = planes // PART
    for q in range(parts):
        for copy in ready(q):
            copy.start()

    for copy in rates:
        copy.wait()

    for p in range(planes):
        hcol[p : p + 1, :] = jnp.full((1, half), hz[p // levels, p % levels], jnp.float32)

    for copy in strips:
        copy.wait()
    mine_first, mine_last, before, after = mine.at[0], mine.at[1], halo.at[0], halo.at[1]
    for j in range(4):
        aux[j : j + 1, :] = jnp.full((1, width), (hz[0, 0], hz[0, 1], vt[0], vt[0])[j], jnp.float32)
    aux[4:5, :] = before[1, planes : planes + 1, :]
    aux[5:6, :] = after[0, planes : planes + 1, :]

    level = row_ids(levels, width)
    for side, (x2, x1, x0, m) in enumerate(
        (
            (before.at[0], before.at[1], mine_first.at[0], before[1, planes : planes + 1, :]),
            (after.at[1], after.at[0], mine_last.at[1], after[0, planes : planes + 1, :]),
        )
    ):
        for f in range(fields):
            at = pl.ds(f * levels, levels)
            x = x1[at, :]
            lap = x2[at, :] + x0[at, :] + beside(x)
            below = jnp.where(level == 0, x, pltpu.roll(x, 1, 0))
            above = jnp.where(level == levels - 1, x, pltpu.roll(x, levels - 1, 0))
            h = jnp.concatenate([hcol[at, :]] * 2, 1)
            v = vt[f]
            new = x * (1.0 - 4.0 * h - 2.0 * v) + h * lap + v * (above + below)
            edge[side, at, :] = new * m

    row = row_ids(8, width)
    top, bottom = row == 0, row == 7
    nrow = rows // 8

    for k, lanes in enumerate(sides):
        split[k] = mask[:, lanes]
        for r in range(nrow):
            wet[pl.ds(8 * r, 8), lanes] = split[k, pl.ds(r, 8, stride=nrow), :]

    def pack(p):
        for r in range(nrow):
            s0[p, pl.ds(8 * r, 8), :] = jnp.concatenate([raw[k, p, pl.ds(r, 8, stride=nrow), :] for k in range(2)], 1)

    def substep(src, p, lo, hi, ahead, behind):
        f = p // levels
        h, v = hz[f, p % levels], vt[f]
        c0 = 1.0 - 4.0 * h - 2.0 * v
        x = [src[p, pl.ds(8 * r, 8), :] for r in range(nrow)]
        above = jnp.where(top, jnp.broadcast_to(ahead[pl.ds(p, 1), :], (8, width)), pltpu.roll(x[-1], 1, 0))
        under = jnp.where(bottom, jnp.broadcast_to(behind[pl.ds(p, 1), :], (8, width)), pltpu.roll(x[0], 7, 0))
        for r in range(nrow):
            at = pl.ds(8 * r, 8)
            near = (x[r - 1] if r else above) + (x[r + 1] if r < nrow - 1 else under)
            vert = src[lo, at, :] + src[hi, at, :]
            new = x[r] * c0 + h * (near + beside(x[r])) + v * vert
            yield r, new * wet[at, :]

    def first(start, i):
        p = start + i
        pack(p + 1 if i < BLOCK - 1 else jnp.minimum(p + 1, planes - 1))
        lo = p - 1 if i else jnp.where(p % levels == 0, p, p - 1)
        hi = p + 1 if i < BLOCK - 1 else jnp.where(p % levels == levels - 1, p, p + 1)
        for r, new in substep(s0, p, lo, hi, before.at[1], after.at[0]):
            s1[p, pl.ds(8 * r, 8), :] = new

    def second_at(p, lo, hi):
        for r, new in substep(s1, p, lo, hi, edge.at[0], edge.at[1]):
            for k in range(2):
                res[k, p, pl.ds(r, 8, stride=nrow), :] = new[:, k * half : (k + 1) * half]

    def second(start, i):
        p = start + i - 1 if i else jnp.maximum(start - 1, 0)
        lo = p - 1 if i > 1 else jnp.where(p % levels == 0, p, p - 1)
        hi = p + 1 if i else jnp.where(p % levels == levels - 1, p, p + 1)
        second_at(p, lo, hi)

    for copy in ready(0):
        copy.wait()
    pack(0)
    for i in range(BLOCK):
        if i and i % PART == 0:
            for copy in ready(i // PART):
                copy.wait()
        first(0, i)

    @pl.loop(1, blocks)
    def _(q):
        for j in range(BLOCK // PART - 1):
            for copy in ready(q * (BLOCK // PART) + j):
                copy.wait()

        @pl.when(q < blocks - 1)
        def _():
            for copy in ready((q + 1) * (BLOCK // PART) - 1):
                copy.wait()

        @pl.when(q == blocks - 1)
        def _():
            for copy in ready(parts - 1):
                copy.wait()

        now = q * BLOCK
        for i in range(BLOCK):
            second(now - BLOCK, i)
        for i in range(BLOCK):
            first(now, i)

        @pl.when(q > 1)
        def _():
            leave(now - BLOCK - 1, BLOCK)

        @pl.when(q == 1)
        def _():
            leave(0, BLOCK - 1)
            for k, lanes in enumerate(sides):
                base[:, :, lanes] = res[k, 0:3]

    done = planes - BLOCK - 1
    for i in range(BLOCK):
        second(planes - BLOCK, i)
        if i in (BLOCK // 2, 3 * BLOCK // 4):
            leave(done, planes - BLOCK + i - done)
            done = planes - BLOCK + i
    second_at(planes - 1, planes - 2, planes - 1)
    leave(done, planes - done)
    for copy in store(pl.ds(0, planes)):
        copy.wait()


def mix(fields, hz, vt, sent_near, sent_far, got_near, got_far, mask):
    nf, levels, rows, width = fields.shape
    planes = nf * levels
    flat = (planes, rows, width)
    vmem = pl.BlockSpec(memory_space=pltpu.VMEM)
    hbm = pl.BlockSpec(memory_space=pltpu.HBM)
    halved = (2, planes, rows, width // 2)
    whole, base, aux = pl.pallas_call(
        mix_kernel,
        out_shape=(
            jax.ShapeDtypeStruct(flat, jnp.float32),
            jax.ShapeDtypeStruct((3, rows, width), jnp.float32),
            jax.ShapeDtypeStruct((8, width), jnp.float32),
        ),
        in_specs=[hbm, hbm, hbm, vmem, vmem, vmem, vmem, vmem],
        out_specs=(hbm, vmem, vmem),
        scratch_shapes=[
            pltpu.VMEM((2, 2, planes + 8, width), jnp.float32),
            pltpu.VMEM((2, 2, planes + 8, width), jnp.float32),
            pltpu.SemaphoreType.DMA((4,)),
            pltpu.SMEM((nf, levels), jnp.float32),
            pltpu.SMEM((nf,), jnp.float32),
            pltpu.VMEM((planes, width // 2), jnp.float32),
            pltpu.VMEM(halved, jnp.float32),
            pltpu.VMEM(flat, jnp.float32),
            pltpu.VMEM(flat, jnp.float32),
            pltpu.VMEM(halved, jnp.float32),
            pltpu.VMEM((2, planes, width), jnp.float32),
            pltpu.VMEM((2, rows, width // 2), jnp.float32),
            pltpu.VMEM((rows, width), jnp.float32),
            pltpu.SemaphoreType.DMA((2,)),
            pltpu.SemaphoreType.DMA((planes // PART, 2)),
            pltpu.SemaphoreType.DMA((2,)),
        ],
        compiler_params=pltpu.CompilerParams(vmem_limit_bytes=46 * MIB),
        cost_estimate=pl.CostEstimate(flops=26 * fields.size, bytes_accessed=8 * fields.size, transcendentals=0),
        name="mix",
    )(hz, vt, fields.reshape(flat), sent_near, sent_far, got_near, got_far, mask)
    return whole.reshape(fields.shape), base, aux


def prep_kernel(state, coef_hbm, sea_hbm, out, wet, surface, coef, sea, sem):
    rows, width = coef.shape
    half = width // 2
    copies = [
        pltpu.make_async_copy(state.at[0, 0], surface, sem.at[0]),
        pltpu.make_async_copy(coef_hbm, coef, sem.at[1]),
        pltpu.make_async_copy(sea_hbm, sea, sem.at[2]),
    ]
    for copy in copies:
        copy.start()
    for copy in copies:
        copy.wait()
    ocean = sea[...].astype(jnp.float32)
    mine = lax.axis_index("comp") == 0
    second = jnp.where(mine, coef[...], ocean)
    wet[...] = jnp.where(mine, jnp.ones_like(ocean), ocean)
    for k in range(2):
        lanes = slice(k * half, (k + 1) * half)
        out[pl.ds(2 * k * rows, rows, stride=2), :] = surface[:, lanes]
        out[pl.ds(2 * k * rows + 1, rows, stride=2), :] = second[:, lanes]


def prep(fields, coef, sea):
    vmem = pl.BlockSpec(memory_space=pltpu.VMEM)
    hbm = pl.BlockSpec(memory_space=pltpu.HBM)
    rows, width = coef.shape
    return pl.pallas_call(
        prep_kernel,
        out_shape=(
            jax.ShapeDtypeStruct((4 * rows, width // 2), jnp.float32),
            jax.ShapeDtypeStruct((rows, width), jnp.float32),
        ),
        in_specs=[hbm, hbm, hbm],
        out_specs=(vmem, vmem),
        scratch_shapes=[
            pltpu.VMEM((rows, width), jnp.float32),
            pltpu.VMEM((rows, width), jnp.float32),
            pltpu.VMEM((rows, width), jnp.int32),
            pltpu.SemaphoreType.DMA((3,)),
        ],
        compiler_params=pltpu.CompilerParams(vmem_limit_bytes=60 * MIB),
        cost_estimate=pl.CostEstimate(flops=3 * coef.size, bytes_accessed=24 * coef.size, transcendentals=0),
        name="prep",
    )(fields, coef, sea)


def edge_kernel(state, sea_any, partner_any, near, far, chosen, stage, sea, partner, sem):
    nf, levels, rows, width = state.shape
    planes = nf * levels
    copies = [
        pltpu.make_async_copy(state.at[f, :, pl.ds(at, 8), :], stage.at[side, f], sem.at[side, f])
        for side, at in enumerate((0, rows - 8))
        for f in range(nf)
    ]
    small = [
        pltpu.make_async_copy(sea_any, sea, sem.at[2, 0]),
        pltpu.make_async_copy(partner_any, partner, sem.at[2, 1]),
    ]
    for copy in small + copies:
        copy.start()
    for copy in small:
        copy.wait()
    tiles = chosen.shape[0]
    column = lax.broadcasted_iota(jnp.int32, (1, tiles), 1)
    for t in range(tiles):
        chosen[t : t + 1, :] = (column == partner[t]).astype(jnp.float32)

    def fill(first, last):
        for side, (out, at) in enumerate(((first, 0), (last, 6))):
            for f in range(nf):
                copies[side * nf + f].wait()
                for j in range(2):
                    for g in range(0, levels, 8):
                        p = f * levels + g
                        out[j, p : p + 8, :] = stage[side, f, g : g + 8, at + j, :]
            for j in range(2):
                row = side * (rows - 2) + j
                wet = jnp.where(lax.axis_index("comp") == 0, 1.0, sea[row : row + 1, :].astype(jnp.float32))
                out[j, planes : planes + 8, :] = jnp.broadcast_to(wet, (8, width))

    even = lax.axis_index("tile") % 2 == 0

    @pl.when(even)
    def _():
        fill(far, near)

    @pl.when(jnp.logical_not(even))
    def _():
        fill(near, far)


def edges(fields, sea, partner):
    vmem = pl.BlockSpec(memory_space=pltpu.VMEM)
    anyw = pl.BlockSpec(memory_space=pl.ANY)
    hbm = pl.BlockSpec(memory_space=pltpu.HBM)
    nf, levels, _, width = fields.shape
    shape = jax.ShapeDtypeStruct((2, nf * levels + 8, width), jnp.float32)
    return pl.pallas_call(
        edge_kernel,
        out_shape=(shape, shape, jax.ShapeDtypeStruct((partner.size, partner.size), jnp.float32)),
        in_specs=[hbm, anyw, anyw],
        out_specs=(vmem, vmem, vmem),
        scratch_shapes=[
            pltpu.VMEM((2, nf, levels, 8, width), jnp.float32),
            pltpu.VMEM(sea.shape, jnp.int32),
            pltpu.SMEM(partner.shape, jnp.int32),
            pltpu.SemaphoreType.DMA((3, nf)),
        ],
        compiler_params=pltpu.CompilerParams(vmem_limit_bytes=46 * MIB),
        cost_estimate=pl.CostEstimate(flops=0, bytes_accessed=4 * MIB, transcendentals=0),
        name="edges",
    )(fields, sea, partner)


def flux_kernel(chosen, got, back):
    tiles = chosen.shape[0]
    odd, even = pl.ds(1, tiles, stride=2), pl.ds(0, tiles, stride=2)
    ocean, wet = (got[pl.ds(2 * tiles + k, tiles, stride=2), :] for k in range(2))
    theirs = jnp.dot(chosen[...], ocean, precision=lax.Precision.HIGHEST, preferred_element_type=jnp.float32)
    sea = jnp.dot(chosen[...], wet, preferred_element_type=jnp.float32)
    flux = got[odd, :] * (got[even, :] - theirs) * sea
    turned = lax.dot_general(
        chosen[...], flux, (((0,), (0,)), ((), ())), precision=lax.Precision.HIGHEST, preferred_element_type=jnp.float32
    )
    shift = jnp.where(lax.axis_index("tile") < 2, tiles - 1, 1)
    back[even, :] = flux
    back[odd, :] = pltpu.roll(flux, shift, 0)
    back[pl.ds(2 * tiles, tiles, stride=2), :] = turned
    back[pl.ds(2 * tiles + 1, tiles, stride=2), :] = pltpu.roll(turned, shift, 0)


def flux_pieces(chosen, got):
    vmem = pl.BlockSpec(memory_space=pltpu.VMEM)
    return pl.pallas_call(
        flux_kernel,
        out_shape=jax.ShapeDtypeStruct(got.shape, jnp.float32),
        in_specs=[vmem, vmem],
        out_specs=vmem,
        compiler_params=pltpu.CompilerParams(vmem_limit_bytes=2 * MIB),
        cost_estimate=pl.CostEstimate(flops=3 * 10**10, bytes_accessed=8 * got.size, transcendentals=0),
        name="flux",
    )(chosen, got)


def add_kernel(base, back, mask, aux, whole, out, ext, three, sem):
    del whole
    rows, width = mask.shape
    half = width // 2
    s = jnp.where(lax.axis_index("comp") == 0, -1.0, 1.0).astype(jnp.float32)
    h0, h1, v = (aux[j : j + 1, :] for j in range(3))
    zero_pad = jnp.zeros((8, width), jnp.float32)
    ext[0:8, :] = zero_pad
    ext[8 + rows : 16 + rows, :] = zero_pad
    for k in range(2):
        lanes = pl.ds(k * half, half)
        at = 2 * k * rows
        ext[8 : 8 + rows, lanes] = back[pl.ds(at, rows, stride=2), :] * s
        for j in range(2):
            ext[6 + j : 7 + j, lanes] = back[pl.ds(at + 2 * (rows - 2 + j) + 1, 1), :] * s
            ext[8 + rows + j : 9 + rows + j, lanes] = back[pl.ds(at + 2 * j + 1, 1), :] * s

    total = rows + 16
    m = jnp.concatenate(
        [jnp.broadcast_to(aux[4:5, :], (8, width)), mask[...], jnp.broadcast_to(aux[5:6, :], (8, width))], 0
    )

    def lateral(x):
        return pltpu.roll(x, 1, 0) + pltpu.roll(x, total - 1, 0) + beside(x)

    d = ext[...]
    one0 = m * ((1.0 - 4.0 * h0 - v) * d + h0 * lateral(d))
    one1 = m * (v * d)
    copies = []

    def finish(level, two):
        three[level] = base[level] + (m * two)[8 : 8 + rows]
        copy = pltpu.make_async_copy(three.at[level], out.at[0, level], sem.at[level])
        copy.start()
        copies.append(copy)

    finish(2, v * one1)
    finish(1, (1.0 - 4.0 * h1 - 2.0 * v) * one1 + h1 * lateral(one1) + v * one0)
    finish(0, (1.0 - 4.0 * h0 - v) * one0 + h0 * lateral(one0) + v * one1)
    for copy in copies:
        copy.wait()


def add_flux(base, back, mask, aux, whole):
    vmem = pl.BlockSpec(memory_space=pltpu.VMEM)
    hbm = pl.BlockSpec(memory_space=pltpu.HBM)
    rows, width = mask.shape
    return pl.pallas_call(
        add_kernel,
        out_shape=jax.ShapeDtypeStruct(whole.shape, jnp.float32),
        in_specs=[vmem, vmem, vmem, vmem, hbm],
        out_specs=hbm,
        scratch_shapes=[pltpu.VMEM((rows + 16, width), jnp.float32), pltpu.VMEM(base.shape, jnp.float32), pltpu.SemaphoreType.DMA((3,))],
        input_output_aliases={4: 0},
        compiler_params=pltpu.CompilerParams(vmem_limit_bytes=2 * MIB),
        cost_estimate=pl.CostEstimate(flops=30 * mask.size, bytes_accessed=32 * mask.size, transcendentals=0),
        name="add",
    )(base, back, mask, aux, whole)


def per_device(state, horiz_rate, vert_rate, sea_mask, exchange_coef, partner):
    ntile = lax.axis_size("tile")
    fields, hz, vt = state[0], horiz_rate[0], vert_rate[0]
    outgoing, scale = prep(fields, exchange_coef, sea_mask)
    got = lax.all_to_all(outgoing, BOTH, 0, 0, tiled=True)
    sent_near, sent_far, chosen = edges(fields, sea_mask, partner)
    pieces = flux_pieces(chosen, got)
    back = lax.all_to_all(pieces, BOTH, 0, 0, tiled=True)

    got_near = lax.ppermute(sent_near, "tile", [(i, i ^ 1) for i in range(ntile)])
    got_far = lax.ppermute(sent_far, "tile", [(i, (i + 2 * (i % 2) - 1) % ntile) for i in range(ntile)])
    whole, base, aux = mix(fields, hz, vt, sent_near, sent_far, got_near, got_far, scale)
    return add_flux(base, back, scale, aux, whole)[None]


def solution(mesh):
    placed = (
        P("comp", None, None, "tile", None),
        P("comp", None, None),
        P("comp", None),
        P("tile", None),
        P("tile", None),
        P(),
    )
    return jax.shard_map(
        per_device,
        mesh=mesh,
        in_specs=placed,
        out_specs=P("comp", None, None, "tile", None),
        check_vma=False,
    )
```
